32 devices in a mesh: groups: 2 (over y), rows: 4 (over z), cols: 4 (over x, core).
Axes of the slice: x: 2, y: 2, z: 4, core: 2. Of those that a mesh axis runs over, the one named last changes fastest.
Arguments:
- density: bfloat16 [384, 64, 1600], P(('groups', 'rows', 'cols')), parts along dimension 0, as said below
- columns: int32 [384, 25], P(('groups', 'rows', 'cols')), parts along dimension 0, may hold values from 0 to 191, as said below
- counts: int32 [384], P(('groups', 'rows', 'cols')), parts along dimension 0, may hold values from 1 to 25, as said below
Outputs:
- purified: bfloat16 [384, 64, 1600], P(('groups', 'rows', 'cols')), parts along dimension 0
The draws below stay inside these ranges and needn't reach their ends.
There are 2 independent parts, one for each index of `groups`. The reference program is written for one: setup_inputs(seed, part) draws one part's arguments, and reference() takes and returns one part's arrays. A program takes and returns all parts, laid end to end along the dimension named above; each array names one. Nothing has to cross between parts.
Inputs may be any that keep to these rules, and one draw needn't show every extreme that they name: Row i lists each of the 25 block columns (i + d) mod 192, d = -12 .. 12, exactly once; its first counts[i] entries are the live ones. Liveness is symmetric: column k is live in row i exactly when column i is live in row k, and the diagonal block of every row is live. `counts`: equals the number of live block columns of the row. `density`: the matrix is symmetric: the block in slot 12 + d of row i is the transpose of the block in slot 12 - d of row (i + d) mod 192.
All inputs are finite; a program needn't handle non-finite values.
Results may differ from the reference program's by a relative error of at most 0.0045.
Values may be sent and summed in bfloat16 or wider, within the bound.
No kernel may reach another device: no remote copies, remote signals or barrier semaphores. Data moves between devices by JAX's collectives and lax.ppermute only.
A program may use at most 128 MiB of HBM per device.

```python
import jax
import jax.numpy as jnp
from jax import lax

BLOCK = 64
REACH = 12
WIN = 25
NB = 192


def pattern_of(key):
    slot_count = 2 * REACH + 1
    row_ids = jnp.arange(NB, dtype=jnp.int32)[:, None]
    links = jax.random.randint(key, (NB, REACH), 0, 25) >= 2
    chosen = jax.random.randint(jax.random.fold_in(key, 1), (), 0, NB)
    distance = jnp.arange(1, REACH + 1, dtype=jnp.int32)[None, :]
    forced = (row_ids == chosen) | ((row_ids + distance) % NB == chosen)
    links = links | forced
    offsets = jnp.arange(slot_count, dtype=jnp.int32)[None, :] - REACH
    anchor = (row_ids + jnp.minimum(offsets, 0)) % NB
    reach_idx = jnp.clip(jnp.abs(offsets) - 1, 0, REACH - 1)
    live_slot = jnp.where(offsets == 0, True, links[anchor, reach_idx])
    scores = jax.random.randint(jax.random.fold_in(key, 2), (NB, slot_count), 0, 2 ** 20) * slot_count + offsets + REACH
    ranked = jnp.argsort(jnp.where(live_slot, 0, 2 ** 26) + scores, axis=1)
    listed = (row_ids + ranked.astype(jnp.int32) - REACH) % NB
    totals = jnp.sum(live_slot.astype(jnp.int32), axis=1)
    return (listed.astype(jnp.int32), totals.astype(jnp.int32))


def draw_columns(key, part):
    listed, totals = pattern_of(key)
    return listed


def draw_counts(key, part):
    listed, totals = pattern_of(key)
    return totals


def draw_density(key, part):
    key = jax.random.fold_in(key, 7)
    slot_count = 2 * REACH + 1
    draw_shape = (NB, REACH + 1, BLOCK, BLOCK)
    base_blocks = jax.random.normal(key, draw_shape, jnp.float32)
    factors = jnp.ones((NB,), jnp.float32)
    diagonal = 0.7071 * (base_blocks[:, 0] + jnp.swapaxes(base_blocks[:, 0], 1, 2))
    base_blocks = jnp.concatenate([diagonal[:, None], base_blocks[:, 1:]], axis=1)
    offsets = jnp.arange(slot_count, dtype=jnp.int32) - REACH
    row_ids = jnp.arange(NB, dtype=jnp.int32)[:, None]
    anchor = (row_ids + jnp.minimum(offsets, 0)[None, :]) % NB
    picked = base_blocks[anchor, jnp.abs(offsets)[None, :]]
    picked = jnp.where((offsets < 0)[None, :, None, None], jnp.swapaxes(picked, 2, 3), picked)
    weights = 0.06 * factors[anchor]
    values = picked * weights[:, :, None, None]
    return jnp.transpose(values, (0, 2, 1, 3)).reshape(NB, BLOCK, slot_count * BLOCK).astype(jnp.bfloat16)


def setup_inputs(seed: int = 0, part: int = 0) -> dict:
    arg_keys = jax.random.split(jax.random.key(seed), 4)
    part_splits = jax.random.split(jax.random.fold_in(arg_keys[3], part), 4)
    return {
        "density": draw_density(jax.random.fold_in(jax.random.fold_in(arg_keys[3], part), 71), part),
        "columns": draw_columns(jax.random.fold_in(jax.random.fold_in(arg_keys[3], part), 71), part),
        "counts": draw_counts(jax.random.fold_in(jax.random.fold_in(arg_keys[3], part), 71), part),
    }


def live_slots(columns, counts, row_ids):
    slot_count = columns.shape[1]
    offsets = jnp.arange(slot_count, dtype=jnp.int32) - REACH
    wanted = (row_ids[:, None] + offsets[None, :]) % NB
    listed = jnp.arange(slot_count, dtype=jnp.int32)[None, :] < counts[:, None]
    matches = (columns[:, None, :] == wanted[:, :, None]) & listed[:, None, :]
    return jnp.any(matches, axis=2)


def masked_blocks(values, live_slot):
    row_count = values.shape[0]
    shaped = values.reshape(row_count, BLOCK, WIN, BLOCK)
    kept_blocks = jnp.where(live_slot[:, None, :, None], shaped, jnp.zeros_like(shaped))
    return kept_blocks.reshape(row_count, BLOCK, WIN * BLOCK)


def banded_product(left_rows, right_rows, live_slot):
    slot_idx = jnp.arange(WIN, dtype=jnp.int32)
    source = slot_idx[None, :] - slot_idx[:, None] + REACH
    inside = (source >= 0) & (source < WIN)
    source = jnp.clip(source, 0, WIN - 1)
    source_full = jnp.broadcast_to(source[:, None, :, None], (WIN, BLOCK, WIN, BLOCK))

    def one_row(row_index):
        needed = (row_index + slot_idx - REACH) % NB
        blocks = right_rows[needed].reshape(WIN, BLOCK, WIN, BLOCK)
        picked = jnp.take_along_axis(blocks, source_full, axis=2)
        picked = jnp.where(inside[:, None, :, None], picked, jnp.zeros_like(picked))
        return jnp.dot(left_rows[row_index], picked.reshape(WIN * BLOCK, WIN * BLOCK), preferred_element_type=jnp.float32)

    summed = lax.map(one_row, jnp.arange(NB, dtype=jnp.int32))
    shaped = summed.reshape(NB, BLOCK, WIN, BLOCK)
    kept_blocks = jnp.where(live_slot[:, None, :, None], shaped, jnp.zeros_like(shaped))
    return kept_blocks.reshape(NB, BLOCK, WIN * BLOCK)


def reference(density, columns, counts):
    row_ids = jnp.arange(NB, dtype=jnp.int32)
    live_slot = live_slots(columns, counts, row_ids)
    kept_blocks = masked_blocks(density, live_slot)
    square = banded_product(kept_blocks, kept_blocks, live_slot).astype(jnp.bfloat16)
    cube_term = banded_product(kept_blocks, square, live_slot)
    return (3.0 * square.astype(jnp.float32) - 2.0 * cube_term).astype(jnp.bfloat16)
```

```python
import jax
import jax.numpy as jnp
from jax import lax
from jax.experimental import pallas as pl
from jax.experimental.pallas import tpu as pltpu
from jax.sharding import PartitionSpec as P

BS = 64
ROWS = 12
SLOTS = 25
OWN = ROWS * BS
WIDE = 3 * OWN
T = 256
NT = OWN // T
MB = 128
NM = OWN // MB
PACKED = (NM * (NM - 1) // 2 + NM // 2) * MB + 16
RING = ("rows", "cols")
F32 = jnp.float32
BF16 = jnp.bfloat16


def dot_nn(a, b):
    return lax.dot_general(a, b, (((1,), (0,)), ((), ())), preferred_element_type=F32)


def dot_nt(a, b):
    return lax.dot_general(a, b, (((1,), (1,)), ((), ())), preferred_element_type=F32)


def live_lanes(cols_ref, counts_ref, all_rows, first_block, blocks):
    first_row = lax.axis_index(RING) * ROWS
    slot = lax.broadcasted_iota(jnp.int32, (ROWS, SLOTS), 1)
    row = lax.broadcasted_iota(jnp.int32, (ROWS, SLOTS), 0)
    limit = jnp.zeros((ROWS, SLOTS), jnp.int32)
    for r in range(ROWS):
        limit = jnp.where(row == r, counts_ref[r], limit)
    local = cols_ref[...] - (first_row - ROWS)
    local = jnp.where(local < 0, local + all_rows, local)
    local = jnp.where(local >= all_rows, local - all_rows, local)
    local = jnp.where(slot < limit, local, -1)
    block = lax.shift_right_logical(
        lax.broadcasted_iota(jnp.int32, (ROWS, blocks * BS), 1), 6
    ) + first_block
    live = jnp.zeros((ROWS, blocks * BS), F32)
    for e in range(SLOTS):
        live = jnp.where(local[:, e : e + 1] == block, 1.0, live)
    return live


def triangle_slots():
    at, n = {}, 0
    for a in range(NM):
        for b in range(a + 1, NM):
            at[a, b] = n
            n += 1
    return at, n


def pack_triangle(macro, out_ref):
    at, n = triangle_slots()
    for (a, b), k in at.items():
        out_ref[k * MB : (k + 1) * MB, :] = macro(a, b)
    row = lax.broadcasted_iota(jnp.int32, (MB, MB), 0)
    col = lax.broadcasted_iota(jnp.int32, (MB, MB), 1)
    tail = jnp.zeros((16, MB), F32)
    tail_row = lax.broadcasted_iota(jnp.int32, (16, MB), 0)
    for h in range(NM // 2):
        first = macro(2 * h, 2 * h).astype(F32)
        second = macro(2 * h + 1, 2 * h + 1).astype(F32)
        k = n + h
        out_ref[k * MB : (k + 1) * MB, :] = jnp.where(row <= col, first, second).astype(BF16)
        diagonal = jnp.sum(jnp.where(row == col, second, 0.0), axis=0, keepdims=True)
        tail = jnp.where(tail_row == h, diagonal, tail)
    out_ref[(n + NM // 2) * MB :, :] = tail.astype(BF16)


def unpack_triangle(in_ref, out_ref):
    at, n = triangle_slots()
    for (a, b), k in at.items():
        value = in_ref[k * MB : (k + 1) * MB, :]
        out_ref[a * MB : (a + 1) * MB, b * MB : (b + 1) * MB] = value
        out_ref[b * MB : (b + 1) * MB, a * MB : (a + 1) * MB] = value.T
    row = lax.broadcasted_iota(jnp.int32, (MB, MB), 0)
    col = lax.broadcasted_iota(jnp.int32, (MB, MB), 1)
    tail = in_ref[(n + NM // 2) * MB :, :].astype(F32)
    for h in range(NM // 2):
        k = n + h
        value = in_ref[k * MB : (k + 1) * MB, :].astype(F32)
        turned = value.T
        first = jnp.where(row <= col, value, turned)
        second = jnp.where(row > col, value, jnp.where(row < col, turned, tail[h : h + 1, :]))
        a, b = 2 * h, 2 * h + 1
        out_ref[a * MB : (a + 1) * MB, a * MB : (a + 1) * MB] = first.astype(BF16)
        out_ref[b * MB : (b + 1) * MB, b * MB : (b + 1) * MB] = second.astype(BF16)


def pack_kernel(all_rows, dens_ref, cols_ref, counts_ref, out_ref, buf, sem):
    copy = pltpu.make_async_copy(dens_ref.at[:, :, pl.ds(640, 896)], buf, sem)
    copy.start()
    live = live_lanes(cols_ref, counts_ref, all_rows, ROWS, ROWS).astype(BF16)
    copy.wait()

    def macro(a, b):
        even, odd = 2 * a, 2 * a + 1
        mask = live[:, b * MB : (b + 1) * MB]
        at = (b - a + 1) * MB
        top = buf[even, :, at : at + MB] * mask[even : even + 1]
        wide = buf[odd, :, at - MB : at + MB]
        low = wide[:, BS : BS + MB] * mask[odd : odd + 1]
        return jnp.concatenate([top, low], axis=0)

    pack_triangle(macro, out_ref)


def mask_tile(live_ref, i, col, width=T):
    rows = [
        jnp.broadcast_to(live_ref[r : r + 1, col : col + width], (BS, width))
        for r in range(i * T // BS, (i + 1) * T // BS)
    ]
    return jnp.concatenate(rows, axis=0) > 0.0


def square_kernel(all_rows, dens_ref, cols_ref, counts_ref, dense_ref, sd_ref, pack_ref, live_ref):
    live = live_lanes(cols_ref, counts_ref, all_rows, 0, 3 * ROWS)
    live_ref[0:ROWS, :] = live
    live_ref[ROWS:, :] = jnp.zeros((16 - ROWS, WIDE), F32)
    live16 = live.astype(BF16)
    panel = SLOTS * BS
    for r in range(ROWS):
        at = (r // 2) * MB
        rows = slice(r * BS, (r + 1) * BS)
        value = dens_ref[r]
        pad = jnp.zeros((BS, BS), BF16)
        pieces = [value, pad] if r % 2 == 0 else [pad, value]
        value = jnp.concatenate(pieces, axis=1)
        value = value * live16[r : r + 1, at : at + panel + BS]
        if at:
            dense_ref[rows, 0:at] = jnp.zeros((BS, at), BF16)
        dense_ref[rows, at : at + panel + BS] = value
        if at + panel + BS < WIDE:
            dense_ref[rows, at + panel + BS :] = jnp.zeros((BS, WIDE - at - panel - BS), BF16)
    for i in range(NT):
        for j in range(NT):
            lo, hi = max(i, j) * T, 2 * OWN + (min(i, j) + 1) * T
            acc = dot_nt(
                dense_ref[i * T : (i + 1) * T, lo:hi], dense_ref[j * T : (j + 1) * T, lo:hi]
            )
            acc = jnp.where(mask_tile(live_ref, i, OWN + j * T), acc, 0.0)
            sd_ref[i * T : (i + 1) * T, j * T : (j + 1) * T] = acc.astype(BF16)

    pack_triangle(
        lambda a, b: sd_ref[a * MB : (a + 1) * MB, b * MB : (b + 1) * MB], pack_ref
    )


def tile(ref, i, j, base=0):
    return ref[i * T : (i + 1) * T, base + j * T : base + (j + 1) * T]


EDGE = MB
GW = OWN + EDGE


def main_kernel(
    dense_ref, sd_ref, live_ref, pc_ref, ps_ref, ss_ref, out_ref, g_ref,
    tl, tr, dl, dr, sn, sl, sr, od,
):
    core = lax.rem(lax.axis_index("cols"), 2)

    @pl.when(core == 1)
    def _():
        tr[...] = pc_ref[...]
        tl[...] = ps_ref[...]

    @pl.when(core == 0)
    def _():
        tr[...] = ps_ref[...]
        tl[...] = pc_ref[...]

    unpack_triangle(tl, dl)
    unpack_triangle(tr, dr)
    unpack_triangle(ss_ref, sn)
    D = OWN
    R = 2 * OWN

    for i in range(NT):
        for j in range(i + 1):
            acc = dot_nn(
                dense_ref[i * T : (i + 1) * T, D + j * T : D + OWN],
                dense_ref[j * T : OWN, R + j * T : R + (j + 1) * T],
            )
            acc += dot_nn(
                dense_ref[i * T : (i + 1) * T, R : R + (i + 1) * T],
                dr[0 : (i + 1) * T, j * T : (j + 1) * T],
            )
            acc = jnp.where(mask_tile(live_ref, i, R + j * T), acc, 0.0)
            sr[i * T : (i + 1) * T, j * T : (j + 1) * T] = acc.astype(BF16)
        for j in range(i, NT):
            acc = dot_nn(
                dense_ref[i * T : (i + 1) * T, D : D + (j + 1) * T],
                dense_ref[0 : (j + 1) * T, j * T : (j + 1) * T],
            )
            acc += dot_nn(
                dense_ref[i * T : (i + 1) * T, i * T : OWN],
                dl[i * T : OWN, j * T : (j + 1) * T],
            )
            acc = jnp.where(mask_tile(live_ref, i, j * T), acc, 0.0)
            sl[i * T : (i + 1) * T, j * T : (j + 1) * T] = acc.astype(BF16)

    def result(i, col, square, cube):
        value = 3.0 * square.astype(F32) - 2.0 * cube
        return jnp.where(mask_tile(live_ref, i, col), value, 0.0)

    for i in range(NT):
        rows = slice(i * T, (i + 1) * T)
        for j in range(NT):
            m, n = max(i, j), min(i, j) + 1
            acc = dot_nn(dense_ref[rows, D : D + OWN], sd_ref[:, j * T : (j + 1) * T])
            acc += dot_nt(dense_ref[rows, m * T : OWN], sl[j * T : (j + 1) * T, m * T : OWN])
            acc += dot_nt(dense_ref[rows, R : R + n * T], sr[j * T : (j + 1) * T, 0 : n * T])
            value = result(i, D + j * T, tile(sd_ref, i, j), acc)
            od[rows, D + j * T : D + (j + 1) * T] = value.astype(BF16)

    def right(i, j):
        return dot_nn(
            dense_ref[i * T : (i + 1) * T, D + j * T : D + OWN],
            sr[j * T : OWN, j * T : (j + 1) * T],
        )

    def left(i, j):
        return dot_nn(
            dense_ref[i * T : (i + 1) * T, D : D + (j + 1) * T],
            sl[0 : (j + 1) * T, j * T : (j + 1) * T],
        )

    @pl.when(core == 1)
    def _():
        for i in range(NT):
            rows = slice(i * T, (i + 1) * T)
            g_ref[rows, 0:EDGE] = od[rows, R - EDGE : R].astype(F32)
            for j in range(i + 1):
                value = 3.0 * tile(sr, i, j).astype(F32) - 2.0 * right(i, j)
                g_ref[rows, EDGE + j * T : EDGE + (j + 1) * T] = value
                od[rows, R + j * T : R + (j + 1) * T] = jnp.zeros((T, T), BF16)
            for j in range(i, NT):
                acc = left(i, j) + dot_nn(
                    dense_ref[rows, i * T : OWN], sn[i * T : OWN, j * T : (j + 1) * T]
                )
                value = result(i, j * T, tile(sl, i, j), acc)
                od[rows, j * T : (j + 1) * T] = value.astype(BF16)

    @pl.when(core == 0)
    def _():
        for i in range(NT):
            rows = slice(i * T, (i + 1) * T)
            g_ref[rows, OWN:] = od[rows, D : D + EDGE].astype(F32)
            for j in range(i, NT):
                value = 3.0 * tile(sl, i, j).astype(F32) - 2.0 * left(i, j)
                g_ref[rows, j * T : (j + 1) * T] = value
                od[rows, j * T : (j + 1) * T] = jnp.zeros((T, T), BF16)
            for j in range(i + 1):
                acc = right(i, j) + dot_nn(
                    dense_ref[rows, R : R + (i + 1) * T], sn[0 : (i + 1) * T, j * T : (j + 1) * T]
                )
                value = result(i, R + j * T, tile(sr, i, j), acc)
                od[rows, R + j * T : R + (j + 1) * T] = value.astype(BF16)

    panel = SLOTS * BS
    for r in range(ROWS):
        at = (r // 2) * MB
        value = od[r * BS : (r + 1) * BS, at : at + panel + BS]
        out_ref[r] = value[:, 0:panel] if r % 2 == 0 else value[:, BS:]


def last_kernel(dense_ref, live_ref, g_ref, sc_ref, part_ref, out_ref, sn, od, band, sem):
    core = lax.rem(lax.axis_index("cols"), 2)
    R = 2 * OWN
    unpack_triangle(sc_ref, sn)

    @pl.when(core == 1)
    def _():
        for i in range(NT):
            rows = slice(i * T, (i + 1) * T)
            od[rows, 0:EDGE] = g_ref[rows, 0:EDGE].astype(BF16)
            for j in range(i + 1):
                acc = dot_nn(
                    dense_ref[rows, R : R + (i + 1) * T], sn[0 : (i + 1) * T, j * T : (j + 1) * T]
                )
                lanes = slice(EDGE + j * T, EDGE + (j + 1) * T)
                value = g_ref[rows, lanes] - 2.0 * acc
                value = jnp.where(mask_tile(live_ref, i, R + j * T), value, 0.0)
                od[rows, lanes] = value.astype(BF16)
        copies = []
        for r in range(ROWS):
            first = 128 * ((24 - r) // 2)
            width = SLOTS * BS - first
            at = first + BS * r - (R - EDGE)
            value = od[r * BS : (r + 1) * BS, at // MB * MB : at + width]
            band[r, :, first:] = value[:, at % MB :]
            copies.append(
                pltpu.make_async_copy(
                    band.at[r, :, pl.ds(first, width)],
                    out_ref.at[r, :, pl.ds(first, width)],
                    sem.at[r],
                )
            )
            copies[-1].start()
        for copy in copies:
            copy.wait()

    @pl.when(core == 0)
    def _():
        for i in range(NT):
            rows = slice(i * T, (i + 1) * T)
            od[rows, OWN:] = g_ref[rows, OWN:].astype(BF16)
            for j in range(i, NT):
                acc = dot_nn(
                    dense_ref[rows, i * T : OWN], sn[i * T : OWN, j * T : (j + 1) * T]
                )
                lanes = slice(j * T, (j + 1) * T)
                value = g_ref[rows, lanes] - 2.0 * acc
                value = jnp.where(mask_tile(live_ref, i, j * T), value, 0.0)
                od[rows, lanes] = value.astype(BF16)
        copies = []
        for r in range(ROWS):
            width = MB * ((12 - r + 1) // 2)
            at = BS * r
            value = od[r * BS : (r + 1) * BS, at // MB * MB : at + width]
            band[r, :, 0:width] = value[:, at % MB :]
            copies.append(
                pltpu.make_async_copy(
                    band.at[r, :, pl.ds(0, width)], out_ref.at[r, :, pl.ds(0, width)], sem.at[r]
                )
            )
            copies[-1].start()
        for copy in copies:
            copy.wait()


VM = pl.BlockSpec(memory_space=pltpu.VMEM)
SM = pl.BlockSpec(memory_space=pltpu.SMEM)
ANY = pl.BlockSpec(memory_space=pl.ANY)


def params():
    return pltpu.CompilerParams(vmem_limit_bytes=40 * 2**20)


def body(density, columns, counts):
    size = lax.axis_size(RING)
    all_rows = ROWS * size
    cross = [(i, (i + 1) % size if i % 2 else (i - 1) % size) for i in range(size)]
    swap = [(i, i + 1 - 2 * (i % 2)) for i in range(size)]
    shape = jax.ShapeDtypeStruct

    def kernel_pack(*refs):
        pack_kernel(all_rows, *refs)

    def kernel_square(*refs):
        square_kernel(all_rows, *refs)

    p_pack = pl.pallas_call(
        kernel_pack,
        out_shape=shape((PACKED, MB), BF16),
        in_specs=[ANY, VM, SM],
        out_specs=VM,
        scratch_shapes=[pltpu.VMEM((ROWS, BS, 896), BF16), pltpu.SemaphoreType.DMA],
        compiler_params=params(),
    )(density, columns, counts)
    p_cross = lax.ppermute(p_pack, RING, cross)
    p_swap = lax.ppermute(p_pack, RING, swap)
    dense, sd, s_pack, live = pl.pallas_call(
        kernel_square,
        out_shape=(
            shape((OWN, WIDE), BF16),
            shape((OWN, OWN), BF16),
            shape((PACKED, MB), BF16),
            shape((16, WIDE), F32),
        ),
        in_specs=[VM, VM, SM],
        out_specs=(VM, VM, VM, VM),
        compiler_params=params(),
    )(density, columns, counts)
    s_cross = lax.ppermute(s_pack, RING, cross)
    s_swap = lax.ppermute(s_pack, RING, swap)
    square_scratch = [pltpu.VMEM((OWN, OWN), BF16)] * 5
    part, g = pl.pallas_call(
        main_kernel,
        out_shape=(shape((ROWS, BS, SLOTS * BS), BF16), shape((OWN, GW), F32)),
        in_specs=[VM] * 6,
        out_specs=(VM, VM),
        scratch_shapes=[pltpu.VMEM((PACKED, MB), BF16)] * 2
        + square_scratch
        + [pltpu.VMEM((OWN, WIDE), BF16)],
        compiler_params=params(),
    )(dense, sd, live, p_cross, p_swap, s_swap)
    return pl.pallas_call(
        last_kernel,
        out_shape=shape((ROWS, BS, SLOTS * BS), BF16),
        in_specs=[VM, VM, VM, VM, ANY],
        out_specs=ANY,
        input_output_aliases={4: 0},
        scratch_shapes=[
            pltpu.VMEM((OWN, OWN), BF16),
            pltpu.VMEM((OWN, GW), BF16),
            pltpu.VMEM((ROWS, BS, SLOTS * BS), BF16),
            pltpu.SemaphoreType.DMA((ROWS,)),
        ],
        compiler_params=params(),
    )(dense, live, g, s_cross, part)


def solution(mesh):
    in_specs = (
        P(("groups", "rows", "cols"), None, None),
        P(("groups", "rows", "cols"), None),
        P(("groups", "rows", "cols")),
    )
    out_specs = P(("groups", "rows", "cols"), None, None)
    return jax.shard_map(body, mesh=mesh, in_specs=in_specs, out_specs=out_specs, check_vma=False)
```

```python
import jax
import jax.numpy as jnp
from jax import lax
from jax.experimental import pallas as pl
from jax.experimental.pallas import tpu as pltpu
from jax.sharding import PartitionSpec as P

BS = 64
ROWS = 12
SLOTS = 25
PANEL = SLOTS * BS
OWN = ROWS * BS
WIDE = 3 * OWN
LEFT, D, RIGHT = 0, OWN, 2 * OWN
T = 256
NT = OWN // T
MB = 128
NM = OWN // MB
PACKED = (NM * (NM - 1) // 2 + NM // 2) * MB + 16
LINKED = (NM * (NM + 1) // 2) * MB
EDGE = MB
GW = OWN + EDGE
RING = ("rows", "cols")
F32 = jnp.float32
BF16 = jnp.bfloat16


def dot_nn(a, b):
    return lax.dot_general(a, b, (((1,), (0,)), ((), ())), preferred_element_type=F32)


def dot_nt(a, b):
    return lax.dot_general(a, b, (((1,), (1,)), ((), ())), preferred_element_type=F32)


def dot_tn(a, b):
    return lax.dot_general(a, b, (((0,), (0,)), ((), ())), preferred_element_type=F32)


def row_span(right, i):
    return slice(0, (i + 1) * T) if right else slice(i * T, OWN)


def col_span(right, j):
    return slice(j * T, OWN) if right else slice(0, (j + 1) * T)


def both_rows(right, i, j):
    return row_span(right, min(i, j) if right else max(i, j))


def both_cols(right, i, j):
    return col_span(right, max(i, j) if right else min(i, j))


def side_tiles(right):
    return [(i, j) for i in range(NT) for j in range(NT) if (j <= i if right else j >= i)]


UPPER = [(i, j) for i in range(NT) for j in range(i, NT)]


def at(i):
    return slice(i * T, (i + 1) * T)


def shift(span, base):
    return slice(span.start + base, span.stop + base)


def base_of(right):
    return RIGHT if right else LEFT


def position():
    ring = lax.axis_index(RING)
    return ring, lax.rem(ring, 2) == 1, lax.rem(lax.div(ring + 1, 2), 2) == 1


def local_blocks(cols_ref, counts_ref, all_rows):
    first_row = lax.axis_index(RING) * ROWS
    slot = lax.broadcasted_iota(jnp.int32, (ROWS, SLOTS), 1)
    row = lax.broadcasted_iota(jnp.int32, (ROWS, SLOTS), 0)
    limit = jnp.zeros((ROWS, SLOTS), jnp.int32)
    for r in range(ROWS):
        limit = jnp.where(row == r, counts_ref[r], limit)
    local = cols_ref[...] - (first_row - ROWS)
    local = jnp.where(local < 0, local + all_rows, local)
    local = jnp.where(local >= all_rows, local - all_rows, local)
    return jnp.where(slot < limit, local, -1)


def live_lanes(local, first_block, lanes, bits):
    block = lax.broadcasted_iota(jnp.int32, (ROWS, lanes), 1)
    block = lax.shift_right_logical(block, bits) + first_block
    live = jnp.zeros((ROWS, lanes), F32)
    for e in range(SLOTS):
        live = jnp.where(local[:, e : e + 1] == block, 1.0, live)
    return live


def triangle_slots():
    at, n = {}, 0
    for a in range(NM):
        for b in range(a + 1, NM):
            at[a, b] = n
            n += 1
    return at, n


def pack_triangle(macro, out_ref, live_small=None):
    at, n = triangle_slots()
    for (a, b), k in at.items():
        out_ref[k * MB : (k + 1) * MB, :] = macro(a, b)
    row = lax.broadcasted_iota(jnp.int32, (MB, MB), 0)
    col = lax.broadcasted_iota(jnp.int32, (MB, MB), 1)
    tail = jnp.zeros((16, MB), F32)
    if live_small is not None:
        tail = jnp.concatenate([jnp.zeros((16 - ROWS, MB), F32), live_small], axis=0)
    tail_row = lax.broadcasted_iota(jnp.int32, (16, MB), 0)
    for h in range(NM // 2):
        first = macro(2 * h, 2 * h).astype(F32)
        second = macro(2 * h + 1, 2 * h + 1).astype(F32)
        k = n + h
        out_ref[k * MB : (k + 1) * MB, :] = jnp.where(row <= col, first, second).astype(BF16)
        diagonal = jnp.sum(jnp.where(row == col, second, 0.0), axis=0, keepdims=True)
        tail = jnp.where(tail_row == h, diagonal, tail)
    out_ref[PACKED - 16 : PACKED, :] = tail.astype(BF16)


def unpack_triangle(in_ref, out_ref):
    at, n = triangle_slots()
    for (a, b), k in at.items():
        value = in_ref[k * MB : (k + 1) * MB, :]
        out_ref[a * MB : (a + 1) * MB, b * MB : (b + 1) * MB] = value
        out_ref[b * MB : (b + 1) * MB, a * MB : (a + 1) * MB] = value.T
    row = lax.broadcasted_iota(jnp.int32, (MB, MB), 0)
    col = lax.broadcasted_iota(jnp.int32, (MB, MB), 1)
    tail = in_ref[PACKED - 16 : PACKED, :].astype(F32)
    for h in range(NM // 2):
        k = n + h
        value = in_ref[k * MB : (k + 1) * MB, :].astype(F32)
        turned = value.T
        first = jnp.where(row <= col, value, turned)
        second = jnp.where(row > col, value, jnp.where(row < col, turned, tail[h : h + 1, :]))
        a, b = 2 * h, 2 * h + 1
        out_ref[a * MB : (a + 1) * MB, a * MB : (a + 1) * MB] = first.astype(BF16)
        out_ref[b * MB : (b + 1) * MB, b * MB : (b + 1) * MB] = second.astype(BF16)


def pack_kernel(
    all_rows, dens_ref, cols_hbm, counts_hbm, out_ref, local_ref, buf, cols, counts, sem
):
    _, odd_core, near = position()
    small = [
        pltpu.make_async_copy(cols_hbm, cols, sem.at[0]),
        pltpu.make_async_copy(counts_hbm, counts, sem.at[1]),
    ]
    for copy in small:
        copy.start()
    right_copies, left_copies = [], []
    for r in range(ROWS):
        first = MB * ((2 * ROWS - r) // 2)
        lanes = pl.ds(first, PANEL - first)
        right_copies.append(
            pltpu.make_async_copy(dens_ref.at[r, :, lanes], buf.at[r, :, lanes], sem.at[2 + r])
        )
        width = MB * ((ROWS - r + 1) // 2)
        left_copies.append(
            pltpu.make_async_copy(
                dens_ref.at[r, :, pl.ds(0, width)], buf.at[r, :, pl.ds(MB, width)], sem.at[2 + r]
            )
        )
    even_core = jnp.logical_not(odd_core)

    def each(copies, what):
        for copy in copies:
            getattr(copy, what)()

    near_even = jnp.logical_and(near, even_core)
    near_odd = jnp.logical_and(near, odd_core)
    pl.when(near_even)(lambda: each(right_copies, "start"))
    pl.when(near_odd)(lambda: each(left_copies, "start"))
    for copy in small:
        copy.wait()
    local = local_blocks(cols, counts, all_rows)
    local_ref[...] = local
    live = live_lanes(local, jnp.where(odd_core, 0, 2 * ROWS), OWN, 6).astype(BF16)
    zero = jnp.zeros((BS, BS), BF16)
    slots, n = triangle_slots()
    order = dict(slots)
    for a in range(NM):
        order[a, a] = n + a

    @pl.when(near_even)
    def _():
        each(right_copies, "wait")
        for (b, a), k in order.items():
            lanes = slice(b * MB, (b + 1) * MB)
            top, low = live[2 * a : 2 * a + 1, lanes], live[2 * a + 1 : 2 * a + 2, lanes]
            s = (ROWS - a + b) * MB
            if a == b:
                even = jnp.concatenate([buf[2 * a, :, s : s + BS] * top[:, 0:BS], zero], axis=1)
            else:
                even = buf[2 * a, :, s : s + MB] * top
            odd = buf[2 * a + 1, :, s - MB : s + (BS if a == b else MB)][:, BS : BS + MB] * low
            out_ref[k * MB : k * MB + BS, :] = even
            out_ref[k * MB + BS : (k + 1) * MB, :] = odd

    @pl.when(near_odd)
    def _():
        each(left_copies, "wait")
        for (a, b), k in order.items():
            lanes = slice(b * MB, (b + 1) * MB)
            top, low = live[2 * a : 2 * a + 1, lanes], live[2 * a + 1 : 2 * a + 2, lanes]
            s = (b - a + 1) * MB
            even = buf[2 * a, :, s : s + MB] * top
            if a == b:
                odd = buf[2 * a + 1, :, s : s + MB][:, 0:BS] * low[:, BS:]
                odd = jnp.concatenate([zero, odd], axis=1)
            else:
                odd = buf[2 * a + 1, :, s - MB : s + MB][:, BS : BS + MB] * low
            out_ref[k * MB : k * MB + BS, :] = even
            out_ref[k * MB + BS : (k + 1) * MB, :] = odd


def unpack_link(in_ref, out_ref, lower):
    slots, n = triangle_slots()
    order = dict(slots)
    for a in range(NM):
        order[a, a] = n + a
    for (a, b), k in order.items():
        i, j = (b, a) if lower else (a, b)
        out_ref[i * MB : (i + 1) * MB, j * MB : (j + 1) * MB] = in_ref[k * MB : (k + 1) * MB, :]
        if i // 2 == j // 2 and i != j:
            out_ref[j * MB : (j + 1) * MB, i * MB : (i + 1) * MB] = jnp.zeros((MB, MB), BF16)


def mask_tile(live_ref, i, col, first=0, width=T):
    rows = [
        jnp.broadcast_to(live_ref[r + first : r + first + 1, col : col + width], (BS, width))
        for r in range(i * T // BS, (i + 1) * T // BS)
    ]
    return jnp.concatenate(rows, axis=0) > 0.0


def dense_kernel(dens_ref, local_ref, dense_ref, pp_ref, live_ref):
    local = local_ref[...]
    live = live_lanes(local, 0, WIDE, 6)
    live_ref[0:ROWS, :] = live
    live_ref[ROWS:, :] = jnp.zeros((16 - ROWS, WIDE), F32)
    live_small = live_lanes(local, ROWS, MB, 0)
    live16 = live.astype(BF16)
    for r in range(ROWS):
        s = (r // 2) * MB
        rows = slice(r * BS, (r + 1) * BS)
        value = dens_ref[r]
        pad = jnp.zeros((BS, BS), BF16)
        value = jnp.concatenate([value, pad] if r % 2 == 0 else [pad, value], axis=1)
        value = value * live16[r : r + 1, s : s + PANEL + BS]
        if s:
            dense_ref[rows, 0:s] = jnp.zeros((BS, s), BF16)
        dense_ref[rows, s : s + PANEL + BS] = value
        if s + PANEL + BS < WIDE:
            dense_ref[rows, s + PANEL + BS :] = jnp.zeros((BS, WIDE - s - PANEL - BS), BF16)
    pack_triangle(
        lambda a, b: dense_ref[a * MB : (a + 1) * MB, D + b * MB : D + (b + 1) * MB],
        pp_ref,
        live_small,
    )


def own_kernel(dense_ref, live_ref, sd_ref, sp_ref, cd_ref, yl_ref, yr_ref, gram_ref):
    _, odd_core, _ = position()
    for i in range(NT):
        for j in range(NT):
            span = slice(max(i, j) * T, 2 * OWN + (min(i, j) + 1) * T)
            acc = dot_nt(dense_ref[at(i), span], dense_ref[at(j), span])
            acc = jnp.where(mask_tile(live_ref, i, D + j * T), acc, 0.0)
            sd_ref[at(i), at(j)] = acc.astype(BF16)
    pack_triangle(lambda a, b: sd_ref[a * MB : (a + 1) * MB, b * MB : (b + 1) * MB], sp_ref)
    for i in range(NT):
        for j in range(NT):
            cd_ref[at(i), at(j)] = dot_nn(dense_ref[at(i), D : D + OWN], sd_ref[:, at(j)])
    for right, y_ref in ((False, yl_ref), (True, yr_ref)):
        base = base_of(right)
        for i, j in side_tiles(right):
            span = col_span(right, j)
            y_ref[at(i), at(j)] = dot_nn(
                dense_ref[at(i), shift(span, D)], dense_ref[span, shift(at(j), base)]
            )

    def gram(right):
        base = base_of(right)
        for i, j in UPPER:
            span = both_cols(right, i, j)
            gram_ref[at(i), at(j)] = dot_tn(
                dense_ref[span, shift(at(i), base)], dense_ref[span, shift(at(j), base)]
            )

    pl.when(odd_core)(lambda: gram(True))
    pl.when(jnp.logical_not(odd_core))(lambda: gram(False))


def square_side(right, dense_ref, live_ref, y_ref, diag, s_ref):
    base = base_of(right)
    for i, j in side_tiles(right):
        span = row_span(right, i)
        acc = y_ref[at(i), at(j)] + dot_nn(dense_ref[at(i), shift(span, base)], diag[span, at(j)])
        acc = jnp.where(mask_tile(live_ref, i, base + j * T), acc, 0.0)
        s_ref[at(i), at(j)] = acc.astype(BF16)


def swap_kernel(
    dense_ref, live_ref, cd_ref, yl_ref, yr_ref, gram_ref, ps_ref, ss_ref, v_ref,
    cd_out, gram_out, od, pn, sn, s, v,
):
    _, odd_core, near = position()
    even_core = jnp.logical_not(odd_core)
    unpack_triangle(ps_ref, pn)
    unpack_triangle(ss_ref, sn)

    def side(right):
        base = base_of(right)
        square_side(right, dense_ref, live_ref, yr_ref if right else yl_ref, pn, s)
        for i in range(NT):
            for j in range(NT):
                span = both_rows(right, i, j)
                cd_out[at(i), at(j)] = cd_ref[at(i), at(j)] + dot_nt(
                    dense_ref[at(i), shift(span, base)], s[at(j), span]
                )
        for i, j in side_tiles(right):
            span = col_span(right, j)
            acc = dot_nn(dense_ref[at(i), shift(span, D)], s[span, at(j)])
            span = row_span(right, i)
            acc += dot_nn(dense_ref[at(i), shift(span, base)], sn[span, at(j)])
            value = 3.0 * s[at(i), at(j)].astype(F32) - 2.0 * acc
            value = jnp.where(mask_tile(live_ref, i, base + j * T), value, 0.0)
            od[at(i), shift(at(j), base)] = value.astype(BF16)
        for i, j in side_tiles(not right):
            if i != j:
                od[at(i), shift(at(j), base)] = jnp.zeros((T, T), BF16)
        other = base_of(not right)
        od[:, other : other + OWN] = jnp.zeros((OWN, OWN), BF16)

    pl.when(even_core)(lambda: side(True))
    pl.when(odd_core)(lambda: side(False))

    def link(right):
        unpack_link(v_ref, v, right)
        for i, j in UPPER:
            span = both_rows(right, i, j)
            gram_out[at(i), at(j)] = gram_ref[at(i), at(j)] + dot_nt(v[at(i), span], v[at(j), span])

    pl.when(jnp.logical_and(near, odd_core))(lambda: link(True))
    pl.when(jnp.logical_and(near, even_core))(lambda: link(False))

    @pl.when(jnp.logical_not(near))
    def _():
        for i, j in UPPER:
            gram_out[at(i), at(j)] = gram_ref[at(i), at(j)]


def finish_gram(gram, far_live, sn):
    for i, j in UPPER:
        value = jnp.where(mask_tile(far_live, i, j * T, 16 - ROWS), gram(i, j), 0.0).astype(BF16)
        sn[at(i), at(j)] = value
        if i != j:
            sn[at(j), at(i)] = value.T


def finish_side(right, dense_ref, live_ref, sn, g, od, base_out):
    base = base_of(right)
    for i, j in side_tiles(right):
        span = row_span(right, i)
        acc = dot_nn(dense_ref[at(i), shift(span, base)], sn[span, at(j)])
        value = g(i, j) - 2.0 * acc
        value = jnp.where(mask_tile(live_ref, i, base + j * T), value, 0.0)
        od[at(i), shift(at(j), base_out)] = value.astype(BF16)


def cross_kernel(
    dense_ref, sd_ref, live_ref, cd_ref, yl_ref, yr_ref, gram_ref, od_in, pc_ref,
    out_ref, g_ref, gram_out, far_live, od, pn, sn, s, band, sem,
):
    _, odd_core, near = position()
    far = jnp.logical_not(near)
    even_core = jnp.logical_not(odd_core)

    unpack_triangle(pc_ref, pn)
    one_hot = lax.shift_right_logical(lax.broadcasted_iota(jnp.int32, (MB, OWN), 1), 6)
    one_hot = (one_hot == lax.broadcasted_iota(jnp.int32, (MB, OWN), 0)).astype(F32).astype(BF16)
    far_live[...] = dot_nn(pc_ref[PACKED - 16 :, :], one_hot)

    def own_tiles(right, i):
        base = base_of(right)
        for j in range(NT):
            span = both_rows(right, i, j)
            acc = cd_ref[at(i), at(j)] + dot_nt(
                dense_ref[at(i), shift(span, base)], s[at(j), span]
            )
            value = 3.0 * sd_ref[at(i), at(j)].astype(F32) - 2.0 * acc
            value = jnp.where(mask_tile(live_ref, i, D + j * T), value, 0.0)
            od[at(i), shift(at(j), D)] = value.astype(BF16)

    def send_rows(i):
        for r in range(i * T // BS, (i + 1) * T // BS):
            first = (r // 2) * MB
            value = od[r * BS : (r + 1) * BS, first : first + PANEL + BS]
            band[r] = value[:, 0:PANEL] if r % 2 == 0 else value[:, BS:]
            pltpu.make_async_copy(band.at[r], out_ref.at[r], sem.at[r]).start()

    def near_side(right):
        base = base_of(right)
        square_side(right, dense_ref, live_ref, yr_ref if right else yl_ref, pn, s)
        finish_gram(
            lambda i, j: gram_ref[at(i), at(j)] + dot_nn(pn[at(i), :], pn[:, at(j)]), far_live, sn
        )
        for i in range(NT):
            own_tiles(right, i)
            for j in range(NT):
                if (i, j) not in side_tiles(right):
                    continue
                span = col_span(right, j)
                acc = dot_nn(dense_ref[at(i), shift(span, D)], s[span, at(j)])
                span = row_span(right, i)
                acc += dot_nn(dense_ref[at(i), shift(span, base)], sn[span, at(j)])
                value = 3.0 * s[at(i), at(j)].astype(F32) - 2.0 * acc
                value = jnp.where(mask_tile(live_ref, i, base + j * T), value, 0.0)
                od[at(i), shift(at(j), base)] = value.astype(BF16)
            send_rows(i)

    def far_side(right):
        square_side(right, dense_ref, live_ref, yr_ref if right else yl_ref, pn, s)
        edge = EDGE if right else 0
        for i in range(NT):
            own_tiles(right, i)
            send_rows(i)
        for i, j in side_tiles(right):
            span = col_span(right, j)
            acc = dot_nn(dense_ref[at(i), shift(span, D)], s[span, at(j)])
            g_ref[at(i), shift(at(j), edge)] = 3.0 * s[at(i), at(j)].astype(F32) - 2.0 * acc
        for i, j in UPPER:
            gram_out[at(i), at(j)] = gram_ref[at(i), at(j)] + dot_nn(pn[at(i), :], pn[:, at(j)])
        if right:
            g_ref[:, 0:EDGE] = od[:, RIGHT - EDGE : RIGHT].astype(F32)
        else:
            g_ref[:, OWN:] = od[:, D : D + EDGE].astype(F32)

    pl.when(jnp.logical_and(near, odd_core))(lambda: near_side(True))
    pl.when(jnp.logical_and(near, even_core))(lambda: near_side(False))
    pl.when(jnp.logical_and(far, odd_core))(lambda: far_side(True))
    pl.when(jnp.logical_and(far, even_core))(lambda: far_side(False))
    for r in range(ROWS):
        pltpu.make_async_copy(band.at[r], out_ref.at[r], sem.at[r]).wait()


def last_kernel(
    dense_ref, live_ref, g_ref, gram_ref, far_live, v_ref, part_ref, out_ref, sn, v, od, band, sem
):
    _, odd_core, near = position()
    far = jnp.logical_not(near)

    def side(right):
        unpack_link(v_ref, v, not right)

        def gram(i, j):
            span = both_cols(not right, i, j)
            return gram_ref[at(i), at(j)] + dot_tn(v[span, at(i)], v[span, at(j)])

        finish_gram(gram, far_live, sn)
        edge = EDGE if right else 0
        finish_side(
            right, dense_ref, live_ref, sn,
            lambda i, j: g_ref[at(i), shift(at(j), edge)], od, edge,
        )
        if right:
            od[:, 0:EDGE] = g_ref[:, 0:EDGE].astype(BF16)
        else:
            od[:, OWN:] = g_ref[:, OWN:].astype(BF16)
        copies = []
        for r in range(ROWS):
            if right:
                first = MB * ((2 * ROWS - r) // 2)
                width = PANEL - first
                begin = first + BS * r - (RIGHT - EDGE)
            else:
                first = 0
                width = MB * ((ROWS - r + 1) // 2)
                begin = BS * r
            value = od[r * BS : (r + 1) * BS, begin // MB * MB : begin + width]
            band[r, :, first : first + width] = value[:, begin % MB :]
            lanes = pl.ds(first, width)
            copies.append(
                pltpu.make_async_copy(band.at[r, :, lanes], out_ref.at[r, :, lanes], sem.at[r])
            )
            copies[-1].start()
        for copy in copies:
            copy.wait()

    pl.when(jnp.logical_and(far, odd_core))(lambda: side(True))
    pl.when(jnp.logical_and(far, jnp.logical_not(odd_core)))(lambda: side(False))


VM = pl.BlockSpec(memory_space=pltpu.VMEM)
HBM = pl.BlockSpec(memory_space=pltpu.HBM)
ANY = pl.BlockSpec(memory_space=pl.ANY)
DMA = pltpu.SemaphoreType.DMA


def cost(tiles):
    return pl.CostEstimate(flops=2 * T**3 * tiles, bytes_accessed=2**20, transcendentals=0)


def params(mib):
    return pltpu.CompilerParams(vmem_limit_bytes=mib * 2**20)


def body(density, columns, counts):
    size = lax.axis_size(RING)
    all_rows = ROWS * size
    cross = [(i, (i + 1) % size if i % 2 else (i - 1) % size) for i in range(size)]
    swap = [(i, i + 1 - 2 * (i % 2)) for i in range(size)]
    near = [(i, i + 1 if i % 4 == 1 else i - 1) for i in range(size) if i % 4 in (1, 2)]
    onward = [
        (i, (i + 3 if i % 4 == 1 else i - 3) % size) for i in range(size) if i % 4 in (1, 2)
    ]
    shape = jax.ShapeDtypeStruct
    full = shape((OWN, OWN), F32)
    own16 = pltpu.VMEM((OWN, OWN), BF16)

    def kernel_pack(*refs):
        pack_kernel(all_rows, *refs)

    hbm = [pltpu.with_memory_space_constraint(x, pltpu.HBM) for x in (density, columns, counts)]
    link, local = pl.pallas_call(
        kernel_pack,
        out_shape=(shape((LINKED, MB), BF16), shape((ROWS, SLOTS), jnp.int32)),
        in_specs=[HBM, HBM, HBM],
        out_specs=(VM, VM),
        scratch_shapes=[
            pltpu.VMEM((ROWS, BS, PANEL), BF16),
            pltpu.VMEM((ROWS, SLOTS), jnp.int32),
            pltpu.SMEM((ROWS,), jnp.int32),
            DMA((2 + ROWS,)),
        ],
        cost_estimate=cost(10),
        compiler_params=params(16),
    )(*hbm)
    v_near = lax.ppermute(link, RING, near)
    dense, p_pack, live = pl.pallas_call(
        dense_kernel,
        out_shape=(shape((OWN, WIDE), BF16), shape((PACKED, MB), BF16), shape((16, WIDE), F32)),
        in_specs=[VM, VM],
        out_specs=(VM,) * 3,
        cost_estimate=cost(10),
        compiler_params=params(16),
    )(density, local)
    sd, s_pack, cd, yl, yr, gram = pl.pallas_call(
        own_kernel,
        out_shape=(
            shape((OWN, OWN), BF16), shape((PACKED, MB), BF16), full, full, full, full,
        ),
        in_specs=[VM, VM],
        out_specs=(VM,) * 6,
        cost_estimate=cost(150),
        compiler_params=params(16),
    )(dense, live)
    p_late, s_late = lax.optimization_barrier((p_pack, s_pack))
    p_cross = lax.ppermute(p_late, RING, cross)
    p_swap = lax.ppermute(p_late, RING, swap)
    s_swap = lax.ppermute(s_late, RING, swap)
    cd, gram, od = pl.pallas_call(
        swap_kernel,
        out_shape=(full, full, shape((OWN, WIDE), BF16)),
        in_specs=[VM] * 9,
        out_specs=(VM,) * 3,
        scratch_shapes=[own16] * 4,
        input_output_aliases={2: 0, 5: 1},
        cost_estimate=cost(70),
        compiler_params=params(20),
    )(dense, live, cd, yl, yr, gram, p_swap, s_swap, v_near)
    v_onward, _ = lax.optimization_barrier((v_near, od))
    v_far = lax.ppermute(v_onward, RING, onward)
    part, g, gram, far_live, _ = pl.pallas_call(
        cross_kernel,
        out_shape=(
            shape((ROWS, BS, PANEL), BF16),
            shape((OWN, GW), F32),
            full,
            shape((16, OWN), F32),
            shape((OWN, WIDE), BF16),
        ),
        in_specs=[VM] * 9,
        out_specs=(HBM, VM, VM, VM, VM),
        scratch_shapes=[own16] * 3
        + [
            pltpu.VMEM((ROWS, BS, PANEL), BF16),
            DMA((ROWS,)),
        ],
        input_output_aliases={6: 2, 7: 4},
        cost_estimate=cost(300),
        compiler_params=params(20),
    )(dense, sd, live, cd, yl, yr, gram, od, p_cross)
    return pl.pallas_call(
        last_kernel,
        out_shape=shape((ROWS, BS, PANEL), BF16),
        in_specs=[VM] * 6 + [HBM],
        out_specs=HBM,
        input_output_aliases={6: 0},
        scratch_shapes=[
            own16,
            own16,
            pltpu.VMEM((OWN, GW), BF16),
            pltpu.VMEM((ROWS, BS, PANEL), BF16),
            DMA((ROWS,)),
        ],
        cost_estimate=cost(1),
        compiler_params=params(20),
    )(dense, live, g, gram, far_live, v_far, part)


def solution(mesh):
    in_specs = (
        P(("groups", "rows", "cols"), None, None),
        P(("groups", "rows", "cols"), None),
        P(("groups", "rows", "cols")),
    )
    out_specs = P(("groups", "rows", "cols"), None, None)
    return jax.shard_map(body, mesh=mesh, in_specs=in_specs, out_specs=out_specs, check_vma=False)
```

```python
import jax
import jax.numpy as jnp
from jax import lax
from jax.experimental import pallas as pl
from jax.experimental.pallas import tpu as pltpu
from jax.sharding import PartitionSpec as P

BS = 64
ROWS = 12
SLOTS = 25
PANEL = SLOTS * BS
OWN = ROWS * BS
WIDE = 3 * OWN
LEFT, D, RIGHT = 0, OWN, 2 * OWN
T = 256
NT = OWN // T
MB = 128
NM = OWN // MB
PACKED = (NM * (NM - 1) // 2 + NM // 2) * MB + 16
DIAGS = NM * (NM - 1) // 2 * MB
LINKED = DIAGS + 4 * MB + BS
EDGE = MB
GW = OWN + EDGE
RING = ("rows", "cols")
F32 = jnp.float32
BF16 = jnp.bfloat16


def dot_nn(a, b):
    return lax.dot_general(a, b, (((1,), (0,)), ((), ())), preferred_element_type=F32)


def dot_nt(a, b):
    return lax.dot_general(a, b, (((1,), (1,)), ((), ())), preferred_element_type=F32)


def dot_tn(a, b):
    return lax.dot_general(a, b, (((0,), (0,)), ((), ())), preferred_element_type=F32)


def row_span(right, i):
    return slice(0, (i + 1) * T) if right else slice(i * T, OWN)


def col_span(right, j):
    return slice(j * T, OWN) if right else slice(0, (j + 1) * T)


def both_rows(right, i, j):
    return row_span(right, min(i, j) if right else max(i, j))


def both_cols(right, i, j):
    return col_span(right, max(i, j) if right else min(i, j))


def side_tiles(right):
    return [(i, j) for i in range(NT) for j in range(NT) if (j <= i if right else j >= i)]


UPPER = [(i, j) for i in range(NT) for j in range(i, NT)]


def at(i):
    return slice(i * T, (i + 1) * T)


def shift(span, base):
    return slice(span.start + base, span.stop + base)


def base_of(right):
    return RIGHT if right else LEFT


def position():
    ring = lax.axis_index(RING)
    return ring, lax.rem(ring, 2) == 1, lax.rem(lax.div(ring + 1, 2), 2) == 1


def local_blocks(cols_ref, counts_ref, all_rows):
    first_row = lax.axis_index(RING) * ROWS
    slot = lax.broadcasted_iota(jnp.int32, (ROWS, SLOTS), 1)
    row = lax.broadcasted_iota(jnp.int32, (ROWS, SLOTS), 0)
    limit = jnp.zeros((ROWS, SLOTS), jnp.int32)
    for r in range(ROWS):
        limit = jnp.where(row == r, counts_ref[r], limit)
    local = cols_ref[...] - (first_row - ROWS)
    local = jnp.where(local < 0, local + all_rows, local)
    local = jnp.where(local >= all_rows, local - all_rows, local)
    return jnp.where(slot < limit, local, -1)


def live_lanes(local, first_block, lanes, bits):
    block = lax.broadcasted_iota(jnp.int32, (ROWS, lanes), 1)
    block = lax.shift_right_logical(block, bits) + first_block
    live = jnp.zeros((ROWS, lanes), F32)
    for e in range(SLOTS):
        live = jnp.where(local[:, e : e + 1] == block, 1.0, live)
    return live


def triangle_slots():
    at, n = {}, 0
    for a in range(NM):
        for b in range(a + 1, NM):
            at[a, b] = n
            n += 1
    return at, n


def pack_triangle(macro, out_ref, live_small=None):
    at, n = triangle_slots()
    for (a, b), k in at.items():
        out_ref[k * MB : (k + 1) * MB, :] = macro(a, b)
    row = lax.broadcasted_iota(jnp.int32, (MB, MB), 0)
    col = lax.broadcasted_iota(jnp.int32, (MB, MB), 1)
    tail = jnp.zeros((16, MB), F32)
    if live_small is not None:
        tail = jnp.concatenate([jnp.zeros((16 - ROWS, MB), F32), live_small], axis=0)
    tail_row = lax.broadcasted_iota(jnp.int32, (16, MB), 0)
    for h in range(NM // 2):
        first = macro(2 * h, 2 * h).astype(F32)
        second = macro(2 * h + 1, 2 * h + 1).astype(F32)
        k = n + h
        out_ref[k * MB : (k + 1) * MB, :] = jnp.where(row <= col, first, second).astype(BF16)
        diagonal = jnp.sum(jnp.where(row == col, second, 0.0), axis=0, keepdims=True)
        tail = jnp.where(tail_row == h, diagonal, tail)
    out_ref[PACKED - 16 : PACKED, :] = tail.astype(BF16)


def unpack_triangle(in_ref, out_ref):
    at, n = triangle_slots()
    for (a, b), k in at.items():
        value = in_ref[k * MB : (k + 1) * MB, :]
        out_ref[a * MB : (a + 1) * MB, b * MB : (b + 1) * MB] = value
        out_ref[b * MB : (b + 1) * MB, a * MB : (a + 1) * MB] = value.T
    row = lax.broadcasted_iota(jnp.int32, (MB, MB), 0)
    col = lax.broadcasted_iota(jnp.int32, (MB, MB), 1)
    tail = in_ref[PACKED - 16 : PACKED, :].astype(F32)
    for h in range(NM // 2):
        k = n + h
        value = in_ref[k * MB : (k + 1) * MB, :].astype(F32)
        turned = value.T
        first = jnp.where(row <= col, value, turned)
        second = jnp.where(row > col, value, jnp.where(row < col, turned, tail[h : h + 1, :]))
        a, b = 2 * h, 2 * h + 1
        out_ref[a * MB : (a + 1) * MB, a * MB : (a + 1) * MB] = first.astype(BF16)
        out_ref[b * MB : (b + 1) * MB, b * MB : (b + 1) * MB] = second.astype(BF16)


def pack_link(rows_of, lower, out_ref):
    slots, _ = triangle_slots()
    for (a, b), k in slots.items():
        even, odd = rows_of(b, a) if lower else rows_of(a, b)
        out_ref[k * MB : k * MB + BS, :] = even
        out_ref[k * MB + BS : (k + 1) * MB, :] = odd
    parts = []
    for m in range(NM):
        even, odd = rows_of(m, m)
        first, last = even[:, 0:BS], odd[:, BS:]
        side = odd[:, 0:BS] if lower else even[:, BS:]
        parts.append((first, side, last))
    spare = list(parts[NM - 2] + parts[NM - 1])
    for m in range(4):
        first, side, last = parts[m]
        if lower:
            even, odd = (first, spare[m]), (side, last)
        else:
            even, odd = (first, side), (spare[m], last)
        k = DIAGS + m * MB
        out_ref[k : k + BS, :] = jnp.concatenate(even, axis=1)
        out_ref[k + BS : k + MB, :] = jnp.concatenate(odd, axis=1)
    out_ref[LINKED - BS :, :] = jnp.concatenate(spare[4:], axis=1)


def unpack_link(in_ref, out_ref, lower):
    slots, _ = triangle_slots()
    for (a, b), k in slots.items():
        i, j = (b, a) if lower else (a, b)
        out_ref[i * MB : (i + 1) * MB, j * MB : (j + 1) * MB] = in_ref[k * MB : (k + 1) * MB, :]
        if i // 2 == j // 2:
            out_ref[j * MB : (j + 1) * MB, i * MB : (i + 1) * MB] = jnp.zeros((MB, MB), BF16)
    zero = jnp.zeros((BS, BS), BF16)
    spare, parts = [], []
    for m in range(4):
        k = DIAGS + m * MB
        even, odd = in_ref[k : k + BS, :], in_ref[k + BS : k + MB, :]
        if lower:
            spare.append(even[:, BS:])
            parts.append((even[:, 0:BS], odd[:, 0:BS], odd[:, BS:]))
        else:
            spare.append(odd[:, 0:BS])
            parts.append((even[:, 0:BS], even[:, BS:], odd[:, BS:]))
    rest = in_ref[LINKED - BS :, :]
    spare += [rest[:, 0:BS], rest[:, BS:]]
    parts += [tuple(spare[0:3]), tuple(spare[3:6])]
    for m, (first, side, last) in enumerate(parts):
        even = (first, zero) if lower else (first, side)
        odd = (side, last) if lower else (zero, last)
        lanes = slice(m * MB, (m + 1) * MB)
        out_ref[m * MB : m * MB + BS, lanes] = jnp.concatenate(even, axis=1)
        out_ref[m * MB + BS : (m + 1) * MB, lanes] = jnp.concatenate(odd, axis=1)


def pack_kernel(
    all_rows, dens_ref, cols_hbm, counts_hbm, out_ref, local_ref, buf, cols, counts, sem
):
    _, odd_core, near = position()
    far = jnp.logical_not(near)
    near_even = jnp.logical_and(near, jnp.logical_not(odd_core))
    near_odd = jnp.logical_and(near, odd_core)
    small = [
        pltpu.make_async_copy(cols_hbm, cols, sem.at[0]),
        pltpu.make_async_copy(counts_hbm, counts, sem.at[1]),
    ]
    for copy in small:
        copy.start()

    def row_copy(r, first, width, to):
        return pltpu.make_async_copy(
            dens_ref.at[r, :, pl.ds(first, width)], buf.at[r, :, pl.ds(to, width)], sem.at[2 + r]
        )

    right_copies, left_copies, own_copies = [], [], []
    for r in range(ROWS):
        first = MB * ((2 * ROWS - r) // 2)
        right_copies.append(row_copy(r, first, PANEL - first, first))
        left_copies.append(row_copy(r, 0, MB * ((ROWS - r + 1) // 2), MB))
        own_copies.append(row_copy(r, OWN - MB, MB * (NM + 1 - r // 2), OWN - MB))

    def each(copies, what):
        for copy in copies:
            getattr(copy, what)()

    pl.when(near_even)(lambda: each(right_copies, "start"))
    pl.when(near_odd)(lambda: each(left_copies, "start"))
    pl.when(far)(lambda: each(own_copies, "start"))
    for copy in small:
        copy.wait()
    local = local_blocks(cols, counts, all_rows)
    local_ref[...] = local
    first_block = jnp.where(far, ROWS, jnp.where(odd_core, 0, 2 * ROWS))
    live = live_lanes(local, first_block, OWN, 6).astype(BF16)
    zero = jnp.zeros((BS, BS), BF16)

    def masks(a, b):
        lanes = slice(b * MB, (b + 1) * MB)
        return live[2 * a : 2 * a + 1, lanes], live[2 * a + 1 : 2 * a + 2, lanes]

    @pl.when(near_even)
    def _():
        each(right_copies, "wait")

        def rows_of(a, b):
            top, low = masks(a, b)
            s = (ROWS - a + b) * MB
            if a == b:
                even = jnp.concatenate([buf[2 * a, :, s : s + BS] * top[:, 0:BS], zero], axis=1)
            else:
                even = buf[2 * a, :, s : s + MB] * top
            odd = buf[2 * a + 1, :, s - MB : s + (BS if a == b else MB)][:, BS : BS + MB] * low
            return even, odd

        pack_link(rows_of, True, out_ref)

    @pl.when(near_odd)
    def _():
        each(left_copies, "wait")

        def rows_of(a, b):
            top, low = masks(a, b)
            s = (b - a + 1) * MB
            even = buf[2 * a, :, s : s + MB] * top
            if a == b:
                odd = buf[2 * a + 1, :, s : s + MB][:, 0:BS] * low[:, BS:]
                odd = jnp.concatenate([zero, odd], axis=1)
            else:
                odd = buf[2 * a + 1, :, s - MB : s + MB][:, BS : BS + MB] * low
            return even, odd

        pack_link(rows_of, False, out_ref)

    @pl.when(far)
    def _():
        each(own_copies, "wait")

        def macro(a, b):
            top, low = masks(a, b)
            s = OWN + (b - a) * MB
            even = buf[2 * a, :, s : s + MB] * top
            odd = buf[2 * a + 1, :, s - MB : s + MB][:, BS : BS + MB] * low
            return jnp.concatenate([even, odd], axis=0)

        pack_triangle(macro, out_ref, live_lanes(local, ROWS, MB, 0))


def mask_tile(live_ref, i, col, first=0, width=T):
    rows = [
        jnp.broadcast_to(live_ref[r + first : r + first + 1, col : col + width], (BS, width))
        for r in range(i * T // BS, (i + 1) * T // BS)
    ]
    return jnp.concatenate(rows, axis=0) > 0.0


def dense_kernel(dens_ref, local_ref, dense_ref, pp_ref, live_ref):
    local = local_ref[...]
    live = live_lanes(local, 0, WIDE, 6)
    live_ref[0:ROWS, :] = live
    live_ref[ROWS:, :] = jnp.zeros((16 - ROWS, WIDE), F32)
    live_small = live_lanes(local, ROWS, MB, 0)
    live16 = live.astype(BF16)
    for r in range(ROWS):
        s = (r // 2) * MB
        rows = slice(r * BS, (r + 1) * BS)
        value = dens_ref[r]
        pad = jnp.zeros((BS, BS), BF16)
        value = jnp.concatenate([value, pad] if r % 2 == 0 else [pad, value], axis=1)
        value = value * live16[r : r + 1, s : s + PANEL + BS]
        if s:
            dense_ref[rows, 0:s] = jnp.zeros((BS, s), BF16)
        dense_ref[rows, s : s + PANEL + BS] = value
        if s + PANEL + BS < WIDE:
            dense_ref[rows, s + PANEL + BS :] = jnp.zeros((BS, WIDE - s - PANEL - BS), BF16)
    pack_triangle(
        lambda a, b: dense_ref[a * MB : (a + 1) * MB, D + b * MB : D + (b + 1) * MB],
        pp_ref,
        live_small,
    )


def own_kernel(dense_ref, live_ref, sd_ref, sp_ref, cd_ref, yl_ref, yr_ref, gram_ref):
    _, odd_core, _ = position()
    for i in range(NT):
        for j in range(NT):
            span = slice(max(i, j) * T, 2 * OWN + (min(i, j) + 1) * T)
            acc = dot_nt(dense_ref[at(i), span], dense_ref[at(j), span])
            acc = jnp.where(mask_tile(live_ref, i, D + j * T), acc, 0.0)
            sd_ref[at(i), at(j)] = acc.astype(BF16)
    pack_triangle(lambda a, b: sd_ref[a * MB : (a + 1) * MB, b * MB : (b + 1) * MB], sp_ref)
    for i in range(NT):
        for j in range(NT):
            cd_ref[at(i), at(j)] = dot_nn(dense_ref[at(i), D : D + OWN], sd_ref[:, at(j)])
    for right, y_ref in ((False, yl_ref), (True, yr_ref)):
        base = base_of(right)
        for i, j in side_tiles(right):
            span = col_span(right, j)
            y_ref[at(i), at(j)] = dot_nn(
                dense_ref[at(i), shift(span, D)], dense_ref[span, shift(at(j), base)]
            )

    def gram(right):
        base = base_of(right)
        for i, j in UPPER:
            span = both_cols(right, i, j)
            gram_ref[at(i), at(j)] = dot_tn(
                dense_ref[span, shift(at(i), base)], dense_ref[span, shift(at(j), base)]
            )

    pl.when(odd_core)(lambda: gram(True))
    pl.when(jnp.logical_not(odd_core))(lambda: gram(False))


def square_side(right, dense_ref, live_ref, y_ref, diag, s_ref):
    base = base_of(right)
    for i, j in side_tiles(right):
        span = row_span(right, i)
        acc = y_ref[at(i), at(j)] + dot_nn(dense_ref[at(i), shift(span, base)], diag[span, at(j)])
        acc = jnp.where(mask_tile(live_ref, i, base + j * T), acc, 0.0)
        s_ref[at(i), at(j)] = acc.astype(BF16)


def swap_kernel(
    dense_ref, live_ref, cd_ref, yl_ref, yr_ref, ps_ref, ss_ref, cd_out, od, pn, sn, s
):
    _, odd_core, _ = position()
    even_core = jnp.logical_not(odd_core)
    unpack_triangle(ps_ref, pn)
    unpack_triangle(ss_ref, sn)

    def side(right):
        base = base_of(right)
        square_side(right, dense_ref, live_ref, yr_ref if right else yl_ref, pn, s)
        for i in range(NT):
            for j in range(NT):
                span = both_rows(right, i, j)
                cd_out[at(i), at(j)] = cd_ref[at(i), at(j)] + dot_nt(
                    dense_ref[at(i), shift(span, base)], s[at(j), span]
                )
        for i, j in side_tiles(right):
            span = col_span(right, j)
            acc = dot_nn(dense_ref[at(i), shift(span, D)], s[span, at(j)])
            span = row_span(right, i)
            acc += dot_nn(dense_ref[at(i), shift(span, base)], sn[span, at(j)])
            value = 3.0 * s[at(i), at(j)].astype(F32) - 2.0 * acc
            value = jnp.where(mask_tile(live_ref, i, base + j * T), value, 0.0)
            od[at(i), shift(at(j), base)] = value.astype(BF16)
        for i, j in side_tiles(not right):
            if i != j:
                od[at(i), shift(at(j), base)] = jnp.zeros((T, T), BF16)
        other = base_of(not right)
        od[:, other : other + OWN] = jnp.zeros((OWN, OWN), BF16)

    pl.when(even_core)(lambda: side(True))
    pl.when(odd_core)(lambda: side(False))


def link_kernel(gram_ref, v_ref, gram_out, v):
    _, odd_core, near = position()
    even_core = jnp.logical_not(odd_core)

    def link(right):
        unpack_link(v_ref, v, right)
        for i, j in UPPER:
            span = both_rows(right, i, j)
            gram_out[at(i), at(j)] = gram_ref[at(i), at(j)] + dot_nt(v[at(i), span], v[at(j), span])

    pl.when(jnp.logical_and(near, odd_core))(lambda: link(True))
    pl.when(jnp.logical_and(near, even_core))(lambda: link(False))


def finish_gram(gram, far_live, sn):
    for i, j in UPPER:
        value = jnp.where(mask_tile(far_live, i, j * T, 16 - ROWS), gram(i, j), 0.0).astype(BF16)
        sn[at(i), at(j)] = value
        if i != j:
            sn[at(j), at(i)] = value.T


def finish_side(right, dense_ref, live_ref, sn, g, od, base_out):
    base = base_of(right)
    for i, j in side_tiles(right):
        span = row_span(right, i)
        acc = dot_nn(dense_ref[at(i), shift(span, base)], sn[span, at(j)])
        value = g(i, j) - 2.0 * acc
        value = jnp.where(mask_tile(live_ref, i, base + j * T), value, 0.0)
        od[at(i), shift(at(j), base_out)] = value.astype(BF16)


def cross_kernel(
    dense_ref, sd_ref, live_ref, cd_ref, yl_ref, yr_ref, gram_ref, od_in, near_ref, far_ref,
    out_ref, g_ref, gram_out, far_live, od, pn, sn, s, band, sem,
):
    _, odd_core, near = position()
    far = jnp.logical_not(near)
    even_core = jnp.logical_not(odd_core)

    one_hot = lax.shift_right_logical(lax.broadcasted_iota(jnp.int32, (MB, OWN), 1), 6)
    one_hot = (one_hot == lax.broadcasted_iota(jnp.int32, (MB, OWN), 0)).astype(F32).astype(BF16)

    def unpack(ref):
        unpack_triangle(ref, pn)
        far_live[...] = dot_nn(ref[PACKED - 16 : PACKED, :], one_hot)

    def own_tiles(right, i):
        base = base_of(right)
        for j in range(NT):
            span = both_rows(right, i, j)
            acc = cd_ref[at(i), at(j)] + dot_nt(
                dense_ref[at(i), shift(span, base)], s[at(j), span]
            )
            value = 3.0 * sd_ref[at(i), at(j)].astype(F32) - 2.0 * acc
            value = jnp.where(mask_tile(live_ref, i, D + j * T), value, 0.0)
            od[at(i), shift(at(j), D)] = value.astype(BF16)

    def send_rows(i):
        for r in range(i * T // BS, (i + 1) * T // BS):
            first = (r // 2) * MB
            value = od[r * BS : (r + 1) * BS, first : first + PANEL + BS]
            band[r] = value[:, 0:PANEL] if r % 2 == 0 else value[:, BS:]
            pltpu.make_async_copy(band.at[r], out_ref.at[r], sem.at[r]).start()

    def near_side(right):
        base = base_of(right)
        unpack(near_ref)
        square_side(right, dense_ref, live_ref, yr_ref if right else yl_ref, pn, s)
        finish_gram(
            lambda i, j: gram_ref[at(i), at(j)] + dot_nn(pn[at(i), :], pn[:, at(j)]), far_live, sn
        )
        for i in range(NT):
            own_tiles(right, i)
            for j in range(NT):
                if (i, j) not in side_tiles(right):
                    continue
                span = col_span(right, j)
                acc = dot_nn(dense_ref[at(i), shift(span, D)], s[span, at(j)])
                span = row_span(right, i)
                acc += dot_nn(dense_ref[at(i), shift(span, base)], sn[span, at(j)])
                value = 3.0 * s[at(i), at(j)].astype(F32) - 2.0 * acc
                value = jnp.where(mask_tile(live_ref, i, base + j * T), value, 0.0)
                od[at(i), shift(at(j), base)] = value.astype(BF16)
            send_rows(i)

    def far_side(right):
        unpack(far_ref)
        square_side(right, dense_ref, live_ref, yr_ref if right else yl_ref, pn, s)
        edge = EDGE if right else 0
        for i in range(NT):
            own_tiles(right, i)
            send_rows(i)
        for i, j in side_tiles(right):
            span = col_span(right, j)
            acc = dot_nn(dense_ref[at(i), shift(span, D)], s[span, at(j)])
            g_ref[at(i), shift(at(j), edge)] = 3.0 * s[at(i), at(j)].astype(F32) - 2.0 * acc
        for i, j in UPPER:
            gram_out[at(i), at(j)] = gram_ref[at(i), at(j)] + dot_nn(pn[at(i), :], pn[:, at(j)])
        if right:
            g_ref[:, 0:EDGE] = od[:, RIGHT - EDGE : RIGHT].astype(F32)
        else:
            g_ref[:, OWN:] = od[:, D : D + EDGE].astype(F32)

    pl.when(jnp.logical_and(near, odd_core))(lambda: near_side(True))
    pl.when(jnp.logical_and(near, even_core))(lambda: near_side(False))
    pl.when(jnp.logical_and(far, odd_core))(lambda: far_side(True))
    pl.when(jnp.logical_and(far, even_core))(lambda: far_side(False))
    for r in range(ROWS):
        pltpu.make_async_copy(band.at[r], out_ref.at[r], sem.at[r]).wait()


def last_kernel(
    dense_ref, live_ref, g_ref, gram_ref, far_live, v_ref, part_ref, out_ref, sn, v, od, band, sem
):
    _, odd_core, near = position()
    far = jnp.logical_not(near)

    def side(right):
        unpack_link(v_ref, v, not right)

        def gram(i, j):
            span = both_cols(not right, i, j)
            return gram_ref[at(i), at(j)] + dot_tn(v[span, at(i)], v[span, at(j)])

        finish_gram(gram, far_live, sn)
        edge = EDGE if right else 0
        finish_side(
            right, dense_ref, live_ref, sn,
            lambda i, j: g_ref[at(i), shift(at(j), edge)], od, edge,
        )
        if right:
            od[:, 0:EDGE] = g_ref[:, 0:EDGE].astype(BF16)
        else:
            od[:, OWN:] = g_ref[:, OWN:].astype(BF16)
        copies = []
        for r in range(ROWS):
            if right:
                first = MB * ((2 * ROWS - r) // 2)
                width = PANEL - first
                begin = first + BS * r - (RIGHT - EDGE)
            else:
                first = 0
                width = MB * ((ROWS - r + 1) // 2)
                begin = BS * r
            value = od[r * BS : (r + 1) * BS, begin // MB * MB : begin + width]
            band[r, :, first : first + width] = value[:, begin % MB :]
            lanes = pl.ds(first, width)
            copies.append(
                pltpu.make_async_copy(band.at[r, :, lanes], out_ref.at[r, :, lanes], sem.at[r])
            )
            copies[-1].start()
        for copy in copies:
            copy.wait()

    pl.when(jnp.logical_and(far, odd_core))(lambda: side(True))
    pl.when(jnp.logical_and(far, jnp.logical_not(odd_core)))(lambda: side(False))


VM = pl.BlockSpec(memory_space=pltpu.VMEM)
HBM = pl.BlockSpec(memory_space=pltpu.HBM)
ANY = pl.BlockSpec(memory_space=pl.ANY)
DMA = pltpu.SemaphoreType.DMA


def cost(tiles):
    return pl.CostEstimate(flops=2 * T**3 * tiles, bytes_accessed=2**20, transcendentals=0)


def params(mib):
    return pltpu.CompilerParams(vmem_limit_bytes=mib * 2**20)


def body(density, columns, counts):
    size = lax.axis_size(RING)
    all_rows = ROWS * size
    cross = [(i, (i + 1) % size if i % 2 else (i - 1) % size) for i in range(size)]
    swap = [(i, i + 1 - 2 * (i % 2)) for i in range(size)]
    near = [(i, i + 1 if i % 4 == 1 else i - 1) for i in range(size) if i % 4 in (1, 2)]
    onward = [
        (i, (i + 3 if i % 4 == 1 else i - 3) % size) for i in range(size) if i % 4 in (1, 2)
    ]
    shape = jax.ShapeDtypeStruct
    full = shape((OWN, OWN), F32)
    own16 = pltpu.VMEM((OWN, OWN), BF16)

    def kernel_pack(*refs):
        pack_kernel(all_rows, *refs)

    hbm = [pltpu.with_memory_space_constraint(x, pltpu.HBM) for x in (density, columns, counts)]
    link, local = pl.pallas_call(
        kernel_pack,
        out_shape=(shape((LINKED, MB), BF16), shape((ROWS, SLOTS), jnp.int32)),
        in_specs=[HBM, HBM, HBM],
        out_specs=(VM, VM),
        scratch_shapes=[
            pltpu.VMEM((ROWS, BS, PANEL), BF16),
            pltpu.VMEM((ROWS, SLOTS), jnp.int32),
            pltpu.SMEM((ROWS,), jnp.int32),
            DMA((2 + ROWS,)),
        ],
        cost_estimate=cost(10),
        compiler_params=params(16),
    )(*hbm)
    first = lax.ppermute(link, RING, cross)
    dense, p_pack, live = pl.pallas_call(
        dense_kernel,
        out_shape=(shape((OWN, WIDE), BF16), shape((PACKED, MB), BF16), shape((16, WIDE), F32)),
        in_specs=[VM, VM],
        out_specs=(VM,) * 3,
        cost_estimate=cost(1),
        compiler_params=params(16),
    )(density, local)
    sd, s_pack, cd, yl, yr, gram = pl.pallas_call(
        own_kernel,
        out_shape=(
            shape((OWN, OWN), BF16), shape((PACKED, MB), BF16), full, full, full, full,
        ),
        in_specs=[VM, VM],
        out_specs=(VM,) * 6,
        cost_estimate=cost(1),
        compiler_params=params(16),
    )(dense, live)
    p_late, s_late = lax.optimization_barrier((p_pack, s_pack))
    p_near = lax.ppermute(p_late, RING, near)
    p_swap = lax.ppermute(p_late, RING, swap)
    s_swap = lax.ppermute(s_late, RING, swap)
    cd, od = pl.pallas_call(
        swap_kernel,
        out_shape=(full, shape((OWN, WIDE), BF16)),
        in_specs=[VM] * 7,
        out_specs=(VM,) * 2,
        scratch_shapes=[own16] * 3,
        input_output_aliases={2: 0},
        cost_estimate=cost(1),
        compiler_params=params(20),
    )(dense, live, cd, yl, yr, p_swap, s_swap)
    v_onward, v, _ = lax.optimization_barrier((first, first, od))
    v_far = lax.ppermute(v_onward, RING, onward)
    gram = pl.pallas_call(
        link_kernel,
        out_shape=full,
        in_specs=[VM] * 2,
        out_specs=VM,
        scratch_shapes=[own16],
        input_output_aliases={0: 0},
        cost_estimate=cost(1),
        compiler_params=params(20),
    )(gram, v)
    part, g, gram, far_live, _ = pl.pallas_call(
        cross_kernel,
        out_shape=(
            shape((ROWS, BS, PANEL), BF16),
            shape((OWN, GW), F32),
            full,
            shape((16, OWN), F32),
            shape((OWN, WIDE), BF16),
        ),
        in_specs=[VM] * 10,
        out_specs=(HBM, VM, VM, VM, VM),
        scratch_shapes=[own16] * 3
        + [
            pltpu.VMEM((ROWS, BS, PANEL), BF16),
            DMA((ROWS,)),
        ],
        input_output_aliases={6: 2, 7: 4},
        cost_estimate=cost(300),
        compiler_params=params(20),
    )(dense, sd, live, cd, yl, yr, gram, od, p_near, first)
    return pl.pallas_call(
        last_kernel,
        out_shape=shape((ROWS, BS, PANEL), BF16),
        in_specs=[VM] * 6 + [HBM],
        out_specs=HBM,
        input_output_aliases={6: 0},
        scratch_shapes=[
            own16,
            own16,
            pltpu.VMEM((OWN, GW), BF16),
            pltpu.VMEM((ROWS, BS, PANEL), BF16),
            DMA((ROWS,)),
        ],
        cost_estimate=cost(1),
        compiler_params=params(20),
    )(dense, live, g, gram, far_live, v_far, part)


def solution(mesh):
    in_specs = (
        P(("groups", "rows", "cols"), None, None),
        P(("groups", "rows", "cols"), None),
        P(("groups", "rows", "cols")),
    )
    out_specs = P(("groups", "rows", "cols"), None, None)
    return jax.shard_map(body, mesh=mesh, in_specs=in_specs, out_specs=out_specs, check_vma=False)
```

```python
import jax
import jax.numpy as jnp
from jax import lax
from jax.experimental import pallas as pl
from jax.experimental.pallas import tpu as pltpu
from jax.sharding import PartitionSpec as P

BS = 64
ROWS = 12
SLOTS = 25
PANEL = SLOTS * BS
OWN = ROWS * BS
WIDE = 3 * OWN
LEFT, D, RIGHT = 0, OWN, 2 * OWN
T = 256
NT = OWN // T
MB = 128
NM = OWN // MB
PACKED = (NM * (NM - 1) // 2 + NM // 2) * MB + 16
DIAGS = NM * (NM - 1) // 2 * MB
LINKED = DIAGS + 4 * MB + BS
EDGE = MB
GW = OWN + EDGE
RING = ("rows", "cols")
F32 = jnp.float32
BF16 = jnp.bfloat16


def dot_nn(a, b):
    return lax.dot_general(a, b, (((1,), (0,)), ((), ())), preferred_element_type=F32)


def dot_nt(a, b):
    return lax.dot_general(a, b, (((1,), (1,)), ((), ())), preferred_element_type=F32)


def dot_tn(a, b):
    return lax.dot_general(a, b, (((0,), (0,)), ((), ())), preferred_element_type=F32)


def row_span(right, i):
    return slice(0, (i + 1) * T) if right else slice(i * T, OWN)


def col_span(right, j):
    return slice(j * T, OWN) if right else slice(0, (j + 1) * T)


def both_rows(right, i, j):
    return row_span(right, min(i, j) if right else max(i, j))


def both_cols(right, i, j):
    return col_span(right, max(i, j) if right else min(i, j))


def side_tiles(right):
    return [(i, j) for i in range(NT) for j in range(NT) if (j <= i if right else j >= i)]


UPPER = [(i, j) for i in range(NT) for j in range(i, NT)]


def at(i):
    return slice(i * T, (i + 1) * T)


def shift(span, base):
    return slice(span.start + base, span.stop + base)


def base_of(right):
    return RIGHT if right else LEFT


def position():
    ring = lax.axis_index(RING)
    return ring, lax.rem(ring, 2) == 1, lax.rem(lax.div(ring + 1, 2), 2) == 1


def local_blocks(cols_ref, counts_ref, all_rows):
    first_row = lax.axis_index(RING) * ROWS
    slot = lax.broadcasted_iota(jnp.int32, (ROWS, SLOTS), 1)
    row = lax.broadcasted_iota(jnp.int32, (ROWS, SLOTS), 0)
    limit = jnp.zeros((ROWS, SLOTS), jnp.int32)
    for r in range(ROWS):
        limit = jnp.where(row == r, counts_ref[r], limit)
    local = cols_ref[...] - (first_row - ROWS)
    local = jnp.where(local < 0, local + all_rows, local)
    local = jnp.where(local >= all_rows, local - all_rows, local)
    return jnp.where(slot < limit, local, -1)


def live_lanes(local, first_block, lanes, bits):
    block = lax.broadcasted_iota(jnp.int32, (ROWS, lanes), 1)
    block = lax.shift_right_logical(block, bits) + first_block
    live = jnp.zeros((ROWS, lanes), F32)
    for e in range(SLOTS):
        live = jnp.where(local[:, e : e + 1] == block, 1.0, live)
    return live


def triangle_slots():
    at, n = {}, 0
    for a in range(NM):
        for b in range(a + 1, NM):
            at[a, b] = n
            n += 1
    return at, n


def pack_triangle(macro, out_ref, live_small=None):
    at, n = triangle_slots()
    for (a, b), k in at.items():
        out_ref[k * MB : (k + 1) * MB, :] = macro(a, b)
    row = lax.broadcasted_iota(jnp.int32, (MB, MB), 0)
    col = lax.broadcasted_iota(jnp.int32, (MB, MB), 1)
    tail = jnp.zeros((16, MB), F32)
    if live_small is not None:
        tail = jnp.concatenate([jnp.zeros((16 - ROWS, MB), F32), live_small], axis=0)
    tail_row = lax.broadcasted_iota(jnp.int32, (16, MB), 0)
    for h in range(NM // 2):
        first = macro(2 * h, 2 * h).astype(F32)
        second = macro(2 * h + 1, 2 * h + 1).astype(F32)
        k = n + h
        out_ref[k * MB : (k + 1) * MB, :] = jnp.where(row <= col, first, second).astype(BF16)
        diagonal = jnp.sum(jnp.where(row == col, second, 0.0), axis=0, keepdims=True)
        tail = jnp.where(tail_row == h, diagonal, tail)
    out_ref[PACKED - 16 : PACKED, :] = tail.astype(BF16)


def unpack_triangle(in_ref, out_ref):
    at, n = triangle_slots()
    for (a, b), k in at.items():
        value = in_ref[k * MB : (k + 1) * MB, :]
        out_ref[a * MB : (a + 1) * MB, b * MB : (b + 1) * MB] = value
        out_ref[b * MB : (b + 1) * MB, a * MB : (a + 1) * MB] = value.T
    row = lax.broadcasted_iota(jnp.int32, (MB, MB), 0)
    col = lax.broadcasted_iota(jnp.int32, (MB, MB), 1)
    tail = in_ref[PACKED - 16 : PACKED, :].astype(F32)
    for h in range(NM // 2):
        k = n + h
        value = in_ref[k * MB : (k + 1) * MB, :].astype(F32)
        turned = value.T
        first = jnp.where(row <= col, value, turned)
        second = jnp.where(row > col, value, jnp.where(row < col, turned, tail[h : h + 1, :]))
        a, b = 2 * h, 2 * h + 1
        out_ref[a * MB : (a + 1) * MB, a * MB : (a + 1) * MB] = first.astype(BF16)
        out_ref[b * MB : (b + 1) * MB, b * MB : (b + 1) * MB] = second.astype(BF16)


def pack_link(rows_of, lower, out_ref):
    slots, _ = triangle_slots()
    for (a, b), k in slots.items():
        even, odd = rows_of(b, a) if lower else rows_of(a, b)
        out_ref[k * MB : k * MB + BS, :] = even
        out_ref[k * MB + BS : (k + 1) * MB, :] = odd
    parts = []
    for m in range(NM):
        even, odd = rows_of(m, m)
        first, last = even[:, 0:BS], odd[:, BS:]
        side = odd[:, 0:BS] if lower else even[:, BS:]
        parts.append((first, side, last))
    spare = list(parts[NM - 2] + parts[NM - 1])
    for m in range(4):
        first, side, last = parts[m]
        if lower:
            even, odd = (first, spare[m]), (side, last)
        else:
            even, odd = (first, side), (spare[m], last)
        k = DIAGS + m * MB
        out_ref[k : k + BS, :] = jnp.concatenate(even, axis=1)
        out_ref[k + BS : k + MB, :] = jnp.concatenate(odd, axis=1)
    out_ref[LINKED - BS :, :] = jnp.concatenate(spare[4:], axis=1)


def unpack_link(in_ref, out_ref, lower):
    slots, _ = triangle_slots()
    for (a, b), k in slots.items():
        i, j = (b, a) if lower else (a, b)
        out_ref[i * MB : (i + 1) * MB, j * MB : (j + 1) * MB] = in_ref[k * MB : (k + 1) * MB, :]
        if i // 2 == j // 2:
            out_ref[j * MB : (j + 1) * MB, i * MB : (i + 1) * MB] = jnp.zeros((MB, MB), BF16)
    zero = jnp.zeros((BS, BS), BF16)
    spare, parts = [], []
    for m in range(4):
        k = DIAGS + m * MB
        even, odd = in_ref[k : k + BS, :], in_ref[k + BS : k + MB, :]
        if lower:
            spare.append(even[:, BS:])
            parts.append((even[:, 0:BS], odd[:, 0:BS], odd[:, BS:]))
        else:
            spare.append(odd[:, 0:BS])
            parts.append((even[:, 0:BS], even[:, BS:], odd[:, BS:]))
    rest = in_ref[LINKED - BS :, :]
    spare += [rest[:, 0:BS], rest[:, BS:]]
    parts += [tuple(spare[0:3]), tuple(spare[3:6])]
    for m, (first, side, last) in enumerate(parts):
        even = (first, zero) if lower else (first, side)
        odd = (side, last) if lower else (zero, last)
        lanes = slice(m * MB, (m + 1) * MB)
        out_ref[m * MB : m * MB + BS, lanes] = jnp.concatenate(even, axis=1)
        out_ref[m * MB + BS : (m + 1) * MB, lanes] = jnp.concatenate(odd, axis=1)


def pack_kernel(
    all_rows, dens_ref, cols_hbm, counts_hbm, out_ref, local_ref, buf, cols, counts, sem
):
    _, odd_core, near = position()
    far = jnp.logical_not(near)
    near_even = jnp.logical_and(near, jnp.logical_not(odd_core))
    near_odd = jnp.logical_and(near, odd_core)
    small = [
        pltpu.make_async_copy(cols_hbm, cols, sem.at[0]),
        pltpu.make_async_copy(counts_hbm, counts, sem.at[1]),
    ]
    for copy in small:
        copy.start()

    def row_copy(r, first, width, to):
        return pltpu.make_async_copy(
            dens_ref.at[r, :, pl.ds(first, width)], buf.at[r, :, pl.ds(to, width)], sem.at[2 + r]
        )

    right_copies, left_copies, own_copies = [], [], []
    for r in range(ROWS):
        first = MB * ((2 * ROWS - r) // 2)
        right_copies.append(row_copy(r, first, PANEL - first, first))
        left_copies.append(row_copy(r, 0, MB * ((ROWS - r + 1) // 2), MB))
        own_copies.append(row_copy(r, OWN - MB, MB * (NM + 1 - r // 2), OWN - MB))

    def each(copies, what):
        for copy in copies:
            getattr(copy, what)()

    pl.when(near_even)(lambda: each(right_copies, "start"))
    pl.when(near_odd)(lambda: each(left_copies, "start"))
    pl.when(far)(lambda: each(own_copies, "start"))
    for copy in small:
        copy.wait()
    local = local_blocks(cols, counts, all_rows)
    local_ref[...] = local
    first_block = jnp.where(far, ROWS, jnp.where(odd_core, 0, 2 * ROWS))
    live = live_lanes(local, first_block, OWN, 6).astype(BF16)
    zero = jnp.zeros((BS, BS), BF16)

    def masks(a, b):
        lanes = slice(b * MB, (b + 1) * MB)
        return live[2 * a : 2 * a + 1, lanes], live[2 * a + 1 : 2 * a + 2, lanes]

    @pl.when(near_even)
    def _():
        each(right_copies, "wait")

        def rows_of(a, b):
            top, low = masks(a, b)
            s = (ROWS - a + b) * MB
            if a == b:
                even = jnp.concatenate([buf[2 * a, :, s : s + BS] * top[:, 0:BS], zero], axis=1)
            else:
                even = buf[2 * a, :, s : s + MB] * top
            odd = buf[2 * a + 1, :, s - MB : s + (BS if a == b else MB)][:, BS : BS + MB] * low
            return even, odd

        pack_link(rows_of, True, out_ref)

    @pl.when(near_odd)
    def _():
        each(left_copies, "wait")

        def rows_of(a, b):
            top, low = masks(a, b)
            s = (b - a + 1) * MB
            even = buf[2 * a, :, s : s + MB] * top
            if a == b:
                odd = buf[2 * a + 1, :, s : s + MB][:, 0:BS] * low[:, BS:]
                odd = jnp.concatenate([zero, odd], axis=1)
            else:
                odd = buf[2 * a + 1, :, s - MB : s + MB][:, BS : BS + MB] * low
            return even, odd

        pack_link(rows_of, False, out_ref)

    @pl.when(far)
    def _():
        each(own_copies, "wait")

        def macro(a, b):
            top, low = masks(a, b)
            s = OWN + (b - a) * MB
            even = buf[2 * a, :, s : s + MB] * top
            odd = buf[2 * a + 1, :, s - MB : s + MB][:, BS : BS + MB] * low
            return jnp.concatenate([even, odd], axis=0)

        pack_triangle(macro, out_ref, live_lanes(local, ROWS, MB, 0))


def mask_tile(live_ref, i, col, first=0, width=T):
    rows = [
        jnp.broadcast_to(live_ref[r + first : r + first + 1, col : col + width], (BS, width))
        for r in range(i * T // BS, (i + 1) * T // BS)
    ]
    return jnp.concatenate(rows, axis=0) > 0.0


def dense_kernel(dens_ref, local_ref, dense_ref, pp_ref, live_ref):
    local = local_ref[...]
    live = live_lanes(local, 0, WIDE, 6)
    live_ref[0:ROWS, :] = live
    live_ref[ROWS:, :] = jnp.zeros((16 - ROWS, WIDE), F32)
    live_small = live_lanes(local, ROWS, MB, 0)
    live16 = live.astype(BF16)
    for r in range(ROWS):
        s = (r // 2) * MB
        rows = slice(r * BS, (r + 1) * BS)
        value = dens_ref[r]
        pad = jnp.zeros((BS, BS), BF16)
        value = jnp.concatenate([value, pad] if r % 2 == 0 else [pad, value], axis=1)
        value = value * live16[r : r + 1, s : s + PANEL + BS]
        if s:
            dense_ref[rows, 0:s] = jnp.zeros((BS, s), BF16)
        dense_ref[rows, s : s + PANEL + BS] = value
        if s + PANEL + BS < WIDE:
            dense_ref[rows, s + PANEL + BS :] = jnp.zeros((BS, WIDE - s - PANEL - BS), BF16)
    pack_triangle(
        lambda a, b: dense_ref[a * MB : (a + 1) * MB, D + b * MB : D + (b + 1) * MB],
        pp_ref,
        live_small,
    )


def own_kernel(dense_ref, live_ref, sd_ref, sp_ref, cd_ref, yl_ref, yr_ref, gram_ref):
    _, odd_core, _ = position()
    for i in range(NT):
        for j in range(NT):
            span = slice(max(i, j) * T, 2 * OWN + (min(i, j) + 1) * T)
            acc = dot_nt(dense_ref[at(i), span], dense_ref[at(j), span])
            acc = jnp.where(mask_tile(live_ref, i, D + j * T), acc, 0.0)
            sd_ref[at(i), at(j)] = acc.astype(BF16)
    pack_triangle(lambda a, b: sd_ref[a * MB : (a + 1) * MB, b * MB : (b + 1) * MB], sp_ref)
    for i in range(NT):
        for j in range(NT):
            cd_ref[at(i), at(j)] = dot_nn(dense_ref[at(i), D : D + OWN], sd_ref[:, at(j)])
    for right, y_ref in ((False, yl_ref), (True, yr_ref)):
        base = base_of(right)
        for i, j in side_tiles(right):
            span = col_span(right, j)
            y_ref[at(i), at(j)] = dot_nn(
                dense_ref[at(i), shift(span, D)], dense_ref[span, shift(at(j), base)]
            )

    def gram(right):
        base = base_of(right)
        for i, j in UPPER:
            span = both_cols(right, i, j)
            gram_ref[at(i), at(j)] = dot_tn(
                dense_ref[span, shift(at(i), base)], dense_ref[span, shift(at(j), base)]
            )

    pl.when(odd_core)(lambda: gram(True))
    pl.when(jnp.logical_not(odd_core))(lambda: gram(False))


def square_side(right, dense_ref, live_ref, y_ref, diag, s_ref):
    base = base_of(right)
    for i, j in side_tiles(right):
        span = row_span(right, i)
        acc = y_ref[at(i), at(j)] + dot_nn(dense_ref[at(i), shift(span, base)], diag[span, at(j)])
        acc = jnp.where(mask_tile(live_ref, i, base + j * T), acc, 0.0)
        s_ref[at(i), at(j)] = acc.astype(BF16)


def swap_kernel(
    dense_ref, live_ref, cd_ref, yl_ref, yr_ref, ps_ref, ss_ref, cd_out, od, pn, sn, s
):
    _, odd_core, _ = position()
    even_core = jnp.logical_not(odd_core)
    unpack_triangle(ps_ref, pn)
    unpack_triangle(ss_ref, sn)

    def side(right):
        base = base_of(right)
        square_side(right, dense_ref, live_ref, yr_ref if right else yl_ref, pn, s)
        for i in range(NT):
            for j in range(NT):
                span = both_rows(right, i, j)
                cd_out[at(i), at(j)] = cd_ref[at(i), at(j)] + dot_nt(
                    dense_ref[at(i), shift(span, base)], s[at(j), span]
                )
        for i, j in side_tiles(right):
            span = col_span(right, j)
            acc = dot_nn(dense_ref[at(i), shift(span, D)], s[span, at(j)])
            span = row_span(right, i)
            acc += dot_nn(dense_ref[at(i), shift(span, base)], sn[span, at(j)])
            value = 3.0 * s[at(i), at(j)].astype(F32) - 2.0 * acc
            value = jnp.where(mask_tile(live_ref, i, base + j * T), value, 0.0)
            od[at(i), shift(at(j), base)] = value.astype(BF16)
        for i, j in side_tiles(not right):
            if i != j:
                od[at(i), shift(at(j), base)] = jnp.zeros((T, T), BF16)
        other = base_of(not right)
        od[:, other : other + OWN] = jnp.zeros((OWN, OWN), BF16)

    pl.when(even_core)(lambda: side(True))
    pl.when(odd_core)(lambda: side(False))


def link_kernel(gram_ref, v_ref, gram_out, v):
    _, odd_core, near = position()
    even_core = jnp.logical_not(odd_core)

    def link(right):
        unpack_link(v_ref, v, right)
        for i, j in UPPER:
            span = both_rows(right, i, j)
            gram_out[at(i), at(j)] = gram_ref[at(i), at(j)] + dot_nt(v[at(i), span], v[at(j), span])

    pl.when(jnp.logical_and(near, odd_core))(lambda: link(True))
    pl.when(jnp.logical_and(near, even_core))(lambda: link(False))


def finish_gram(gram, far_live, sn):
    for i, j in UPPER:
        value = jnp.where(mask_tile(far_live, i, j * T, 16 - ROWS), gram(i, j), 0.0).astype(BF16)
        sn[at(i), at(j)] = value
        if i != j:
            sn[at(j), at(i)] = value.T


def cross_kernel(
    dense_ref, sd_ref, live_ref, cd_ref, yl_ref, yr_ref, gram_ref, od_in, near_ref, far_ref,
    out_ref, g_ref, gram_out, far_live, od, pn, sn, s, band, sem,
):
    _, odd_core, near = position()
    far = jnp.logical_not(near)
    even_core = jnp.logical_not(odd_core)

    one_hot = lax.shift_right_logical(lax.broadcasted_iota(jnp.int32, (MB, OWN), 1), 6)
    one_hot = (one_hot == lax.broadcasted_iota(jnp.int32, (MB, OWN), 0)).astype(F32).astype(BF16)

    def unpack(ref):
        unpack_triangle(ref, pn)
        far_live[...] = dot_nn(ref[PACKED - 16 : PACKED, :], one_hot)

    def own_tiles(right, i):
        base = base_of(right)
        for j in range(NT):
            span = both_rows(right, i, j)
            acc = cd_ref[at(i), at(j)] + dot_nt(
                dense_ref[at(i), shift(span, base)], s[at(j), span]
            )
            value = 3.0 * sd_ref[at(i), at(j)].astype(F32) - 2.0 * acc
            value = jnp.where(mask_tile(live_ref, i, D + j * T), value, 0.0)
            od[at(i), shift(at(j), D)] = value.astype(BF16)

    def send_rows(i):
        for r in range(i * T // BS, (i + 1) * T // BS):
            first = (r // 2) * MB
            value = od[r * BS : (r + 1) * BS, first : first + PANEL + BS]
            band[r] = value[:, 0:PANEL] if r % 2 == 0 else value[:, BS:]
            pltpu.make_async_copy(band.at[r], out_ref.at[r], sem.at[r]).start()

    def near_side(right):
        base = base_of(right)
        unpack(near_ref)
        square_side(right, dense_ref, live_ref, yr_ref if right else yl_ref, pn, s)
        finish_gram(
            lambda i, j: gram_ref[at(i), at(j)] + dot_nn(pn[at(i), :], pn[:, at(j)]), far_live, sn
        )
        for i in range(NT):
            own_tiles(right, i)
            for j in range(NT):
                if (i, j) not in side_tiles(right):
                    continue
                span = col_span(right, j)
                acc = dot_nn(dense_ref[at(i), shift(span, D)], s[span, at(j)])
                span = row_span(right, i)
                acc += dot_nn(dense_ref[at(i), shift(span, base)], sn[span, at(j)])
                value = 3.0 * s[at(i), at(j)].astype(F32) - 2.0 * acc
                value = jnp.where(mask_tile(live_ref, i, base + j * T), value, 0.0)
                od[at(i), shift(at(j), base)] = value.astype(BF16)
            send_rows(i)

    def far_side(right):
        unpack(far_ref)
        square_side(right, dense_ref, live_ref, yr_ref if right else yl_ref, pn, s)
        edge = EDGE if right else 0
        for i in range(NT):
            own_tiles(right, i)
            send_rows(i)
        for i, j in side_tiles(right):
            span = col_span(right, j)
            acc = dot_nn(dense_ref[at(i), shift(span, D)], s[span, at(j)])
            g_ref[at(i), shift(at(j), edge)] = 3.0 * s[at(i), at(j)].astype(F32) - 2.0 * acc
        for i, j in UPPER:
            gram_out[at(i), at(j)] = gram_ref[at(i), at(j)] + dot_nn(pn[at(i), :], pn[:, at(j)])
        if right:
            g_ref[:, 0:EDGE] = od[:, RIGHT - EDGE : RIGHT].astype(F32)
        else:
            g_ref[:, OWN:] = od[:, D : D + EDGE].astype(F32)

    pl.when(jnp.logical_and(near, odd_core))(lambda: near_side(True))
    pl.when(jnp.logical_and(near, even_core))(lambda: near_side(False))
    pl.when(jnp.logical_and(far, odd_core))(lambda: far_side(True))
    pl.when(jnp.logical_and(far, even_core))(lambda: far_side(False))
    for r in range(ROWS):
        pltpu.make_async_copy(band.at[r], out_ref.at[r], sem.at[r]).wait()


def last_kernel(
    dense_ref, live_ref, g_ref, gram_ref, far_live, v_ref, part_ref, out_ref, sn, v, od, band, sem
):
    _, odd_core, near = position()
    far = jnp.logical_not(near)

    def side(right):
        unpack_link(v_ref, v, not right)

        def gram(i, j):
            span = both_cols(not right, i, j)
            return gram_ref[at(i), at(j)] + dot_tn(v[span, at(i)], v[span, at(j)])

        finish_gram(gram, far_live, sn)
        base = base_of(right)
        edge = EDGE if right else 0
        copies = []
        for i in range(NT) if right else range(NT - 1, -1, -1):
            if right:
                od[at(i), 0:EDGE] = g_ref[at(i), 0:EDGE].astype(BF16)
            else:
                od[at(i), OWN:] = g_ref[at(i), OWN:].astype(BF16)
            for j in range(NT):
                if (i, j) not in side_tiles(right):
                    continue
                span = row_span(right, i)
                acc = dot_nn(dense_ref[at(i), shift(span, base)], sn[span, at(j)])
                value = g_ref[at(i), shift(at(j), edge)] - 2.0 * acc
                value = jnp.where(mask_tile(live_ref, i, base + j * T), value, 0.0)
                od[at(i), shift(at(j), edge)] = value.astype(BF16)
            for r in range(i * T // BS, (i + 1) * T // BS):
                if right:
                    first = MB * ((2 * ROWS - r) // 2)
                    width = PANEL - first
                    begin = first + BS * r - (RIGHT - EDGE)
                else:
                    first = 0
                    width = MB * ((ROWS - r + 1) // 2)
                    begin = BS * r
                value = od[r * BS : (r + 1) * BS, begin // MB * MB : begin + width]
                band[r, :, first : first + width] = value[:, begin % MB :]
                lanes = pl.ds(first, width)
                copies.append(
                    pltpu.make_async_copy(band.at[r, :, lanes], out_ref.at[r, :, lanes], sem.at[r])
                )
                copies[-1].start()
        for copy in copies:
            copy.wait()

    pl.when(jnp.logical_and(far, odd_core))(lambda: side(True))
    pl.when(jnp.logical_and(far, jnp.logical_not(odd_core)))(lambda: side(False))


VM = pl.BlockSpec(memory_space=pltpu.VMEM)
HBM = pl.BlockSpec(memory_space=pltpu.HBM)
ANY = pl.BlockSpec(memory_space=pl.ANY)
DMA = pltpu.SemaphoreType.DMA


def cost(tiles):
    return pl.CostEstimate(flops=2 * T**3 * tiles, bytes_accessed=2**20, transcendentals=0)


def params(mib):
    return pltpu.CompilerParams(vmem_limit_bytes=mib * 2**20)


def body(density, columns, counts):
    size = lax.axis_size(RING)
    all_rows = ROWS * size
    cross = [(i, (i + 1) % size if i % 2 else (i - 1) % size) for i in range(size)]
    swap = [(i, i + 1 - 2 * (i % 2)) for i in range(size)]
    near = [(i, i + 1 if i % 4 == 1 else i - 1) for i in range(size) if i % 4 in (1, 2)]
    hop = (1, 3, -3, -1)
    onward = [(i, (i + hop[i % 4]) % size) for i in range(size)]
    shape = jax.ShapeDtypeStruct
    full = shape((OWN, OWN), F32)
    own16 = pltpu.VMEM((OWN, OWN), BF16)

    def kernel_pack(*refs):
        pack_kernel(all_rows, *refs)

    hbm = [pltpu.with_memory_space_constraint(x, pltpu.HBM) for x in (density, columns, counts)]
    link, local = pl.pallas_call(
        kernel_pack,
        out_shape=(shape((LINKED, MB), BF16), shape((ROWS, SLOTS), jnp.int32)),
        in_specs=[HBM, HBM, HBM],
        out_specs=(VM, VM),
        scratch_shapes=[
            pltpu.VMEM((ROWS, BS, PANEL), BF16),
            pltpu.VMEM((ROWS, SLOTS), jnp.int32),
            pltpu.SMEM((ROWS,), jnp.int32),
            DMA((2 + ROWS,)),
        ],
        cost_estimate=cost(10),
        compiler_params=params(16),
    )(*hbm)
    first = lax.ppermute(link, RING, cross)
    dense, p_pack, live = pl.pallas_call(
        dense_kernel,
        out_shape=(shape((OWN, WIDE), BF16), shape((PACKED, MB), BF16), shape((16, WIDE), F32)),
        in_specs=[VM, VM],
        out_specs=(VM,) * 3,
        cost_estimate=cost(1),
        compiler_params=params(16),
    )(density, local)
    sd, s_pack, cd, yl, yr, gram = pl.pallas_call(
        own_kernel,
        out_shape=(
            shape((OWN, OWN), BF16), shape((PACKED, MB), BF16), full, full, full, full,
        ),
        in_specs=[VM, VM],
        out_specs=(VM,) * 6,
        cost_estimate=cost(1),
        compiler_params=params(16),
    )(dense, live)
    p_late, s_late = lax.optimization_barrier((p_pack, s_pack))
    p_near = lax.ppermute(p_late, RING, near)
    p_swap = lax.ppermute(p_late, RING, swap)
    s_swap = lax.ppermute(s_late, RING, swap)
    cd, od = pl.pallas_call(
        swap_kernel,
        out_shape=(full, shape((OWN, WIDE), BF16)),
        in_specs=[VM] * 7,
        out_specs=(VM,) * 2,
        scratch_shapes=[own16] * 3,
        input_output_aliases={2: 0},
        cost_estimate=cost(1),
        compiler_params=params(20),
    )(dense, live, cd, yl, yr, p_swap, s_swap)
    v_onward, v, _ = lax.optimization_barrier((first, first, od))
    v_far = lax.ppermute(v_onward, RING, onward)
    gram = pl.pallas_call(
        link_kernel,
        out_shape=full,
        in_specs=[VM] * 2,
        out_specs=VM,
        scratch_shapes=[own16],
        input_output_aliases={0: 0},
        cost_estimate=cost(1),
        compiler_params=params(20),
    )(gram, v)
    part, g, gram, far_live, _ = pl.pallas_call(
        cross_kernel,
        out_shape=(
            shape((ROWS, BS, PANEL), BF16),
            shape((OWN, GW), F32),
            full,
            shape((16, OWN), F32),
            shape((OWN, WIDE), BF16),
        ),
        in_specs=[VM] * 10,
        out_specs=(HBM, VM, VM, VM, VM),
        scratch_shapes=[own16] * 3
        + [
            pltpu.VMEM((ROWS, BS, PANEL), BF16),
            DMA((ROWS,)),
        ],
        input_output_aliases={6: 2, 7: 4},
        cost_estimate=cost(300),
        compiler_params=params(20),
    )(dense, sd, live, cd, yl, yr, gram, od, p_near, first)
    return pl.pallas_call(
        last_kernel,
        out_shape=shape((ROWS, BS, PANEL), BF16),
        in_specs=[VM] * 6 + [HBM],
        out_specs=HBM,
        input_output_aliases={6: 0},
        scratch_shapes=[
            own16,
            own16,
            pltpu.VMEM((OWN, GW), BF16),
            pltpu.VMEM((ROWS, BS, PANEL), BF16),
            DMA((ROWS,)),
        ],
        cost_estimate=cost(1),
        compiler_params=params(20),
    )(dense, live, g, gram, far_live, v_far, part)


def solution(mesh):
    in_specs = (
        P(("groups", "rows", "cols"), None, None),
        P(("groups", "rows", "cols"), None),
        P(("groups", "rows", "cols")),
    )
    out_specs = P(("groups", "rows", "cols"), None, None)
    return jax.shard_map(body, mesh=mesh, in_specs=in_specs, out_specs=out_specs, check_vma=False)
```

```python
import jax
import jax.numpy as jnp
from jax import lax
from jax.experimental import pallas as pl
from jax.experimental.pallas import tpu as pltpu
from jax.sharding import PartitionSpec as P

BS = 64
ROWS = 12
SLOTS = 25
PANEL = SLOTS * BS
OWN = ROWS * BS
WIDE = 3 * OWN
LEFT, D, RIGHT = 0, OWN, 2 * OWN
T = 256
NT = OWN // T
MB = 128
NM = OWN // MB
PACKED = (NM * (NM - 1) // 2 + NM // 2) * MB + 16
DIAGS = NM * (NM - 1) // 2 * MB
LINKED = DIAGS + 4 * MB + BS
EDGE = MB
GW = OWN + EDGE
RING = ("rows", "cols")
F32 = jnp.float32
BF16 = jnp.bfloat16


def dot_nn(a, b):
    return lax.dot_general(a, b, (((1,), (0,)), ((), ())), preferred_element_type=F32)


def dot_nt(a, b):
    return lax.dot_general(a, b, (((1,), (1,)), ((), ())), preferred_element_type=F32)


def dot_tn(a, b):
    return lax.dot_general(a, b, (((0,), (0,)), ((), ())), preferred_element_type=F32)


def row_span(right, i):
    return slice(0, (i + 1) * T) if right else slice(i * T, OWN)


def col_span(right, j):
    return slice(j * T, OWN) if right else slice(0, (j + 1) * T)


def both_rows(right, i, j):
    return row_span(right, min(i, j) if right else max(i, j))


def both_cols(right, i, j):
    return col_span(right, max(i, j) if right else min(i, j))


def side_tiles(right):
    return [(i, j) for i in range(NT) for j in range(NT) if (j <= i if right else j >= i)]


UPPER = [(i, j) for i in range(NT) for j in range(i, NT)]


def at(i):
    return slice(i * T, (i + 1) * T)


def shift(span, base):
    return slice(span.start + base, span.stop + base)


def base_of(right):
    return RIGHT if right else LEFT


def position():
    ring = lax.axis_index(RING)
    return ring, lax.rem(ring, 2) == 1, lax.rem(lax.div(ring + 1, 2), 2) == 1


def local_blocks(cols_ref, counts_ref, all_rows):
    first_row = lax.axis_index(RING) * ROWS
    slot = lax.broadcasted_iota(jnp.int32, (ROWS, SLOTS), 1)
    row = lax.broadcasted_iota(jnp.int32, (ROWS, SLOTS), 0)
    limit = jnp.zeros((ROWS, SLOTS), jnp.int32)
    for r in range(ROWS):
        limit = jnp.where(row == r, counts_ref[r], limit)
    local = cols_ref[...] - (first_row - ROWS)
    local = jnp.where(local < 0, local + all_rows, local)
    local = jnp.where(local >= all_rows, local - all_rows, local)
    return jnp.where(slot < limit, local, -1)


def live_lanes(local, first_block, lanes, bits):
    block = lax.broadcasted_iota(jnp.int32, (ROWS, lanes), 1)
    block = lax.shift_right_logical(block, bits) + first_block
    live = jnp.zeros((ROWS, lanes), F32)
    for e in range(SLOTS):
        live = jnp.where(local[:, e : e + 1] == block, 1.0, live)
    return live


def triangle_slots():
    at, n = {}, 0
    for a in range(NM):
        for b in range(a + 1, NM):
            at[a, b] = n
            n += 1
    return at, n


def pack_triangle(macro, out_ref, live_small=None):
    at, n = triangle_slots()
    for (a, b), k in at.items():
        out_ref[k * MB : (k + 1) * MB, :] = macro(a, b)
    row = lax.broadcasted_iota(jnp.int32, (MB, MB), 0)
    col = lax.broadcasted_iota(jnp.int32, (MB, MB), 1)
    tail = jnp.zeros((16, MB), F32)
    if live_small is not None:
        tail = jnp.concatenate([jnp.zeros((16 - ROWS, MB), F32), live_small], axis=0)
    tail_row = lax.broadcasted_iota(jnp.int32, (16, MB), 0)
    for h in range(NM // 2):
        first = macro(2 * h, 2 * h).astype(F32)
        second = macro(2 * h + 1, 2 * h + 1).astype(F32)
        k = n + h
        out_ref[k * MB : (k + 1) * MB, :] = jnp.where(row <= col, first, second).astype(BF16)
        diagonal = jnp.sum(jnp.where(row == col, second, 0.0), axis=0, keepdims=True)
        tail = jnp.where(tail_row == h, diagonal, tail)
    out_ref[PACKED - 16 : PACKED, :] = tail.astype(BF16)


def unpack_triangle(in_ref, out_ref):
    at, n = triangle_slots()
    for (a, b), k in at.items():
        value = in_ref[k * MB : (k + 1) * MB, :]
        out_ref[a * MB : (a + 1) * MB, b * MB : (b + 1) * MB] = value
        out_ref[b * MB : (b + 1) * MB, a * MB : (a + 1) * MB] = value.T
    row = lax.broadcasted_iota(jnp.int32, (MB, MB), 0)
    col = lax.broadcasted_iota(jnp.int32, (MB, MB), 1)
    tail = in_ref[PACKED - 16 : PACKED, :].astype(F32)
    for h in range(NM // 2):
        k = n + h
        value = in_ref[k * MB : (k + 1) * MB, :].astype(F32)
        turned = value.T
        first = jnp.where(row <= col, value, turned)
        second = jnp.where(row > col, value, jnp.where(row < col, turned, tail[h : h + 1, :]))
        a, b = 2 * h, 2 * h + 1
        out_ref[a * MB : (a + 1) * MB, a * MB : (a + 1) * MB] = first.astype(BF16)
        out_ref[b * MB : (b + 1) * MB, b * MB : (b + 1) * MB] = second.astype(BF16)


def pack_link(rows_of, lower, out_ref):
    slots, _ = triangle_slots()
    for (a, b), k in slots.items():
        even, odd = rows_of(b, a) if lower else rows_of(a, b)
        out_ref[k * MB : k * MB + BS, :] = even
        out_ref[k * MB + BS : (k + 1) * MB, :] = odd
    parts = []
    for m in range(NM):
        even, odd = rows_of(m, m)
        first, last = even[:, 0:BS], odd[:, BS:]
        side = odd[:, 0:BS] if lower else even[:, BS:]
        parts.append((first, side, last))
    spare = list(parts[NM - 2] + parts[NM - 1])
    for m in range(4):
        first, side, last = parts[m]
        if lower:
            even, odd = (first, spare[m]), (side, last)
        else:
            even, odd = (first, side), (spare[m], last)
        k = DIAGS + m * MB
        out_ref[k : k + BS, :] = jnp.concatenate(even, axis=1)
        out_ref[k + BS : k + MB, :] = jnp.concatenate(odd, axis=1)
    out_ref[LINKED - BS :, :] = jnp.concatenate(spare[4:], axis=1)


def unpack_link(in_ref, out_ref, lower):
    slots, _ = triangle_slots()
    for (a, b), k in slots.items():
        i, j = (b, a) if lower else (a, b)
        out_ref[i * MB : (i + 1) * MB, j * MB : (j + 1) * MB] = in_ref[k * MB : (k + 1) * MB, :]
        if i // 2 == j // 2:
            out_ref[j * MB : (j + 1) * MB, i * MB : (i + 1) * MB] = jnp.zeros((MB, MB), BF16)
    zero = jnp.zeros((BS, BS), BF16)
    spare, parts = [], []
    for m in range(4):
        k = DIAGS + m * MB
        even, odd = in_ref[k : k + BS, :], in_ref[k + BS : k + MB, :]
        if lower:
            spare.append(even[:, BS:])
            parts.append((even[:, 0:BS], odd[:, 0:BS], odd[:, BS:]))
        else:
            spare.append(odd[:, 0:BS])
            parts.append((even[:, 0:BS], even[:, BS:], odd[:, BS:]))
    rest = in_ref[LINKED - BS :, :]
    spare += [rest[:, 0:BS], rest[:, BS:]]
    parts += [tuple(spare[0:3]), tuple(spare[3:6])]
    for m, (first, side, last) in enumerate(parts):
        even = (first, zero) if lower else (first, side)
        odd = (side, last) if lower else (zero, last)
        lanes = slice(m * MB, (m + 1) * MB)
        out_ref[m * MB : m * MB + BS, lanes] = jnp.concatenate(even, axis=1)
        out_ref[m * MB + BS : (m + 1) * MB, lanes] = jnp.concatenate(odd, axis=1)


def pack_kernel(
    all_rows, dens_ref, cols_hbm, counts_hbm, out_ref, local_ref, buf, cols, counts, sem
):
    _, odd_core, near = position()
    near_even = jnp.logical_and(near, jnp.logical_not(odd_core))
    near_odd = jnp.logical_and(near, odd_core)
    small = [
        pltpu.make_async_copy(cols_hbm, cols, sem.at[0]),
        pltpu.make_async_copy(counts_hbm, counts, sem.at[1]),
    ]
    for copy in small:
        copy.start()

    def row_copy(r, first, width, to):
        return pltpu.make_async_copy(
            dens_ref.at[r, :, pl.ds(first, width)], buf.at[r, :, pl.ds(to, width)], sem.at[2 + r]
        )

    right_copies, left_copies = [], []
    for r in range(ROWS):
        first = MB * ((2 * ROWS - r) // 2)
        right_copies.append(row_copy(r, first, PANEL - first, first))
        left_copies.append(row_copy(r, 0, MB * ((ROWS - r + 1) // 2), MB))

    def each(copies, what):
        for copy in copies:
            getattr(copy, what)()

    pl.when(near_even)(lambda: each(right_copies, "start"))
    pl.when(near_odd)(lambda: each(left_copies, "start"))
    for copy in small:
        copy.wait()
    local = local_blocks(cols, counts, all_rows)
    local_ref[...] = local
    live = live_lanes(local, jnp.where(odd_core, 0, 2 * ROWS), OWN, 6).astype(BF16)
    zero = jnp.zeros((BS, BS), BF16)

    def masks(a, b):
        lanes = slice(b * MB, (b + 1) * MB)
        return live[2 * a : 2 * a + 1, lanes], live[2 * a + 1 : 2 * a + 2, lanes]

    @pl.when(near_even)
    def _():
        each(right_copies, "wait")

        def rows_of(a, b):
            top, low = masks(a, b)
            s = (ROWS - a + b) * MB
            if a == b:
                even = jnp.concatenate([buf[2 * a, :, s : s + BS] * top[:, 0:BS], zero], axis=1)
            else:
                even = buf[2 * a, :, s : s + MB] * top
            odd = buf[2 * a + 1, :, s - MB : s + (BS if a == b else MB)][:, BS : BS + MB] * low
            return even, odd

        pack_link(rows_of, True, out_ref)

    @pl.when(near_odd)
    def _():
        each(left_copies, "wait")

        def rows_of(a, b):
            top, low = masks(a, b)
            s = (b - a + 1) * MB
            even = buf[2 * a, :, s : s + MB] * top
            if a == b:
                odd = buf[2 * a + 1, :, s : s + MB][:, 0:BS] * low[:, BS:]
                odd = jnp.concatenate([zero, odd], axis=1)
            else:
                odd = buf[2 * a + 1, :, s - MB : s + MB][:, BS : BS + MB] * low
            return even, odd

        pack_link(rows_of, False, out_ref)


def mask_tile(live_ref, i, col, first=0, width=T):
    rows = [
        jnp.broadcast_to(live_ref[r + first : r + first + 1, col : col + width], (BS, width))
        for r in range(i * T // BS, (i + 1) * T // BS)
    ]
    return jnp.concatenate(rows, axis=0) > 0.0


def dense_kernel(dens_ref, local_ref, dense_ref, pp_ref, live_ref):
    local = local_ref[...]
    live = live_lanes(local, 0, WIDE, 6)
    live_ref[0:ROWS, :] = live
    live_ref[ROWS:, :] = jnp.zeros((16 - ROWS, WIDE), F32)
    live_small = live_lanes(local, ROWS, MB, 0)
    live16 = live.astype(BF16)
    for r in range(ROWS):
        s = (r // 2) * MB
        rows = slice(r * BS, (r + 1) * BS)
        value = dens_ref[r]
        pad = jnp.zeros((BS, BS), BF16)
        value = jnp.concatenate([value, pad] if r % 2 == 0 else [pad, value], axis=1)
        value = value * live16[r : r + 1, s : s + PANEL + BS]
        if s:
            dense_ref[rows, 0:s] = jnp.zeros((BS, s), BF16)
        dense_ref[rows, s : s + PANEL + BS] = value
        if s + PANEL + BS < WIDE:
            dense_ref[rows, s + PANEL + BS :] = jnp.zeros((BS, WIDE - s - PANEL - BS), BF16)
    pack_triangle(
        lambda a, b: dense_ref[a * MB : (a + 1) * MB, D + b * MB : D + (b + 1) * MB],
        pp_ref,
        live_small,
    )


def own_kernel(dense_ref, live_ref, sd_ref, sp_ref, cd_ref, yl_ref, yr_ref, gram_ref):
    _, odd_core, _ = position()
    for i in range(NT):
        for j in range(NT):
            span = slice(max(i, j) * T, 2 * OWN + (min(i, j) + 1) * T)
            acc = dot_nt(dense_ref[at(i), span], dense_ref[at(j), span])
            acc = jnp.where(mask_tile(live_ref, i, D + j * T), acc, 0.0)
            sd_ref[at(i), at(j)] = acc.astype(BF16)
    pack_triangle(lambda a, b: sd_ref[a * MB : (a + 1) * MB, b * MB : (b + 1) * MB], sp_ref)
    for i in range(NT):
        for j in range(NT):
            cd_ref[at(i), at(j)] = dot_nn(dense_ref[at(i), D : D + OWN], sd_ref[:, at(j)])
    for right, y_ref in ((False, yl_ref), (True, yr_ref)):
        base = base_of(right)
        for i, j in side_tiles(right):
            span = col_span(right, j)
            y_ref[at(i), at(j)] = dot_nn(
                dense_ref[at(i), shift(span, D)], dense_ref[span, shift(at(j), base)]
            )

    def gram(right):
        base = base_of(right)
        for i, j in UPPER:
            span = both_cols(right, i, j)
            gram_ref[at(i), at(j)] = dot_tn(
                dense_ref[span, shift(at(i), base)], dense_ref[span, shift(at(j), base)]
            )

    pl.when(odd_core)(lambda: gram(True))
    pl.when(jnp.logical_not(odd_core))(lambda: gram(False))


def square_side(right, dense_ref, live_ref, y_ref, diag, s_ref):
    base = base_of(right)
    for i, j in side_tiles(right):
        span = row_span(right, i)
        acc = y_ref[at(i), at(j)] + dot_nn(dense_ref[at(i), shift(span, base)], diag[span, at(j)])
        acc = jnp.where(mask_tile(live_ref, i, base + j * T), acc, 0.0)
        s_ref[at(i), at(j)] = acc.astype(BF16)


def swap_kernel(
    dense_ref, live_ref, cd_ref, yl_ref, yr_ref, ps_ref, ss_ref, cd_out, od, pn, sn, s
):
    _, odd_core, _ = position()
    even_core = jnp.logical_not(odd_core)
    unpack_triangle(ps_ref, pn)
    unpack_triangle(ss_ref, sn)

    def side(right):
        base = base_of(right)
        square_side(right, dense_ref, live_ref, yr_ref if right else yl_ref, pn, s)
        for i in range(NT):
            for j in range(NT):
                span = both_rows(right, i, j)
                cd_out[at(i), at(j)] = cd_ref[at(i), at(j)] + dot_nt(
                    dense_ref[at(i), shift(span, base)], s[at(j), span]
                )
        for i, j in side_tiles(right):
            span = col_span(right, j)
            acc = dot_nn(dense_ref[at(i), shift(span, D)], s[span, at(j)])
            span = row_span(right, i)
            acc += dot_nn(dense_ref[at(i), shift(span, base)], sn[span, at(j)])
            value = 3.0 * s[at(i), at(j)].astype(F32) - 2.0 * acc
            value = jnp.where(mask_tile(live_ref, i, base + j * T), value, 0.0)
            od[at(i), shift(at(j), base)] = value.astype(BF16)
        for i, j in side_tiles(not right):
            if i != j:
                od[at(i), shift(at(j), base)] = jnp.zeros((T, T), BF16)
        other = base_of(not right)
        od[:, other : other + OWN] = jnp.zeros((OWN, OWN), BF16)

    pl.when(even_core)(lambda: side(True))
    pl.when(odd_core)(lambda: side(False))


def link_kernel(gram_ref, v_ref, gram_out, v):
    _, odd_core, near = position()
    even_core = jnp.logical_not(odd_core)

    def link(right):
        unpack_link(v_ref, v, right)
        for i, j in UPPER:
            span = both_rows(right, i, j)
            gram_out[at(i), at(j)] = gram_ref[at(i), at(j)] + dot_nt(v[at(i), span], v[at(j), span])

    pl.when(jnp.logical_and(near, odd_core))(lambda: link(True))
    pl.when(jnp.logical_and(near, even_core))(lambda: link(False))


def finish_gram(gram, far_live, sn):
    for i, j in UPPER:
        value = jnp.where(mask_tile(far_live, i, j * T, 16 - ROWS), gram(i, j), 0.0).astype(BF16)
        sn[at(i), at(j)] = value
        if i != j:
            sn[at(j), at(i)] = value.T


def cross_kernel(
    dense_ref, sd_ref, live_ref, cd_ref, yl_ref, yr_ref, gram_ref, od_in, pc_ref,
    out_ref, g_ref, gram_out, far_live, od, pn, sn, s, band, sem,
):
    _, odd_core, near = position()
    far = jnp.logical_not(near)
    even_core = jnp.logical_not(odd_core)

    one_hot = lax.shift_right_logical(lax.broadcasted_iota(jnp.int32, (MB, OWN), 1), 6)
    one_hot = (one_hot == lax.broadcasted_iota(jnp.int32, (MB, OWN), 0)).astype(F32).astype(BF16)

    def unpack(ref):
        unpack_triangle(ref, pn)
        far_live[...] = dot_nn(ref[PACKED - 16 : PACKED, :], one_hot)

    def own_tiles(right, i):
        base = base_of(right)
        for j in range(NT):
            span = both_rows(right, i, j)
            acc = cd_ref[at(i), at(j)] + dot_nt(
                dense_ref[at(i), shift(span, base)], s[at(j), span]
            )
            value = 3.0 * sd_ref[at(i), at(j)].astype(F32) - 2.0 * acc
            value = jnp.where(mask_tile(live_ref, i, D + j * T), value, 0.0)
            od[at(i), shift(at(j), D)] = value.astype(BF16)

    def send_rows(i):
        for r in range(i * T // BS, (i + 1) * T // BS):
            first = (r // 2) * MB
            value = od[r * BS : (r + 1) * BS, first : first + PANEL + BS]
            band[r] = value[:, 0:PANEL] if r % 2 == 0 else value[:, BS:]
            pltpu.make_async_copy(band.at[r], out_ref.at[r], sem.at[r]).start()

    def near_side(right):
        base = base_of(right)
        unpack(pc_ref)
        square_side(right, dense_ref, live_ref, yr_ref if right else yl_ref, pn, s)
        finish_gram(
            lambda i, j: gram_ref[at(i), at(j)] + dot_nn(pn[at(i), :], pn[:, at(j)]), far_live, sn
        )
        for i in range(NT):
            own_tiles(right, i)
            for j in range(NT):
                if (i, j) not in side_tiles(right):
                    continue
                span = col_span(right, j)
                acc = dot_nn(dense_ref[at(i), shift(span, D)], s[span, at(j)])
                span = row_span(right, i)
                acc += dot_nn(dense_ref[at(i), shift(span, base)], sn[span, at(j)])
                value = 3.0 * s[at(i), at(j)].astype(F32) - 2.0 * acc
                value = jnp.where(mask_tile(live_ref, i, base + j * T), value, 0.0)
                od[at(i), shift(at(j), base)] = value.astype(BF16)
            send_rows(i)

    def far_side(right):
        unpack(pc_ref)
        square_side(right, dense_ref, live_ref, yr_ref if right else yl_ref, pn, s)
        edge = EDGE if right else 0
        for i in range(NT):
            own_tiles(right, i)
            send_rows(i)
        for i, j in side_tiles(right):
            span = col_span(right, j)
            acc = dot_nn(dense_ref[at(i), shift(span, D)], s[span, at(j)])
            g_ref[at(i), shift(at(j), edge)] = 3.0 * s[at(i), at(j)].astype(F32) - 2.0 * acc
        for i, j in UPPER:
            gram_out[at(i), at(j)] = gram_ref[at(i), at(j)] + dot_nn(pn[at(i), :], pn[:, at(j)])
        if right:
            g_ref[:, 0:EDGE] = od[:, RIGHT - EDGE : RIGHT].astype(F32)
        else:
            g_ref[:, OWN:] = od[:, D : D + EDGE].astype(F32)

    pl.when(jnp.logical_and(near, odd_core))(lambda: near_side(True))
    pl.when(jnp.logical_and(near, even_core))(lambda: near_side(False))
    pl.when(jnp.logical_and(far, odd_core))(lambda: far_side(True))
    pl.when(jnp.logical_and(far, even_core))(lambda: far_side(False))
    for r in range(ROWS):
        pltpu.make_async_copy(band.at[r], out_ref.at[r], sem.at[r]).wait()


def last_kernel(
    dense_ref, live_ref, g_ref, gram_ref, far_live, v_ref, part_ref, out_ref, sn, v, od, band, sem
):
    _, odd_core, near = position()
    far = jnp.logical_not(near)

    def side(right):
        unpack_link(v_ref, v, not right)

        def gram(i, j):
            span = both_cols(not right, i, j)
            return gram_ref[at(i), at(j)] + dot_tn(v[span, at(i)], v[span, at(j)])

        finish_gram(gram, far_live, sn)
        base = base_of(right)
        edge = EDGE if right else 0
        copies = []
        for i in range(NT) if right else range(NT - 1, -1, -1):
            if right:
                od[at(i), 0:EDGE] = g_ref[at(i), 0:EDGE].astype(BF16)
            else:
                od[at(i), OWN:] = g_ref[at(i), OWN:].astype(BF16)
            for j in range(NT):
                if (i, j) not in side_tiles(right):
                    continue
                span = row_span(right, i)
                acc = dot_nn(dense_ref[at(i), shift(span, base)], sn[span, at(j)])
                value = g_ref[at(i), shift(at(j), edge)] - 2.0 * acc
                value = jnp.where(mask_tile(live_ref, i, base + j * T), value, 0.0)
                od[at(i), shift(at(j), edge)] = value.astype(BF16)
            for r in range(i * T // BS, (i + 1) * T // BS):
                if right:
                    first = MB * ((2 * ROWS - r) // 2)
                    width = PANEL - first
                    begin = first + BS * r - (RIGHT - EDGE)
                else:
                    first = 0
                    width = MB * ((ROWS - r + 1) // 2)
                    begin = BS * r
                value = od[r * BS : (r + 1) * BS, begin // MB * MB : begin + width]
                band[r, :, first : first + width] = value[:, begin % MB :]
                lanes = pl.ds(first, width)
                copies.append(
                    pltpu.make_async_copy(band.at[r, :, lanes], out_ref.at[r, :, lanes], sem.at[r])
                )
                copies[-1].start()
        for copy in copies:
            copy.wait()

    pl.when(jnp.logical_and(far, odd_core))(lambda: side(True))
    pl.when(jnp.logical_and(far, jnp.logical_not(odd_core)))(lambda: side(False))


VM = pl.BlockSpec(memory_space=pltpu.VMEM)
HBM = pl.BlockSpec(memory_space=pltpu.HBM)
ANY = pl.BlockSpec(memory_space=pl.ANY)
DMA = pltpu.SemaphoreType.DMA


def cost(tiles):
    return pl.CostEstimate(flops=2 * T**3 * tiles, bytes_accessed=2**20, transcendentals=0)


def params(mib):
    return pltpu.CompilerParams(vmem_limit_bytes=mib * 2**20)


def body(density, columns, counts):
    size = lax.axis_size(RING)
    all_rows = ROWS * size
    cross = [(i, (i + 1) % size if i % 2 else (i - 1) % size) for i in range(size)]
    swap = [(i, i + 1 - 2 * (i % 2)) for i in range(size)]
    near = [(i, i + 1 if i % 4 == 1 else i - 1) for i in range(size) if i % 4 in (1, 2)]
    hop = (1, 3, -3, -1)
    onward = [(i, (i + hop[i % 4]) % size) for i in range(size)]
    shape = jax.ShapeDtypeStruct
    full = shape((OWN, OWN), F32)
    own16 = pltpu.VMEM((OWN, OWN), BF16)

    def kernel_pack(*refs):
        pack_kernel(all_rows, *refs)

    hbm = [pltpu.with_memory_space_constraint(x, pltpu.HBM) for x in (density, columns, counts)]
    link, local = pl.pallas_call(
        kernel_pack,
        out_shape=(shape((LINKED, MB), BF16), shape((ROWS, SLOTS), jnp.int32)),
        in_specs=[HBM, HBM, HBM],
        out_specs=(VM, VM),
        scratch_shapes=[
            pltpu.VMEM((ROWS, BS, PANEL), BF16),
            pltpu.VMEM((ROWS, SLOTS), jnp.int32),
            pltpu.SMEM((ROWS,), jnp.int32),
            DMA((2 + ROWS,)),
        ],
        cost_estimate=cost(10),
        compiler_params=params(16),
    )(*hbm)
    first = lax.ppermute(link, RING, near)
    dense, p_pack, live = pl.pallas_call(
        dense_kernel,
        out_shape=(shape((OWN, WIDE), BF16), shape((PACKED, MB), BF16), shape((16, WIDE), F32)),
        in_specs=[VM, VM],
        out_specs=(VM,) * 3,
        cost_estimate=cost(1),
        compiler_params=params(16),
    )(density, local)
    sd, s_pack, cd, yl, yr, gram = pl.pallas_call(
        own_kernel,
        out_shape=(
            shape((OWN, OWN), BF16), shape((PACKED, MB), BF16), full, full, full, full,
        ),
        in_specs=[VM, VM],
        out_specs=(VM,) * 6,
        cost_estimate=cost(1),
        compiler_params=params(16),
    )(dense, live)
    p_late, s_late = lax.optimization_barrier((p_pack, s_pack))
    p_cross = lax.ppermute(p_late, RING, cross)
    p_swap = lax.ppermute(p_late, RING, swap)
    s_swap = lax.ppermute(s_late, RING, swap)
    cd, od = pl.pallas_call(
        swap_kernel,
        out_shape=(full, shape((OWN, WIDE), BF16)),
        in_specs=[VM] * 7,
        out_specs=(VM,) * 2,
        scratch_shapes=[own16] * 3,
        input_output_aliases={2: 0},
        cost_estimate=cost(1),
        compiler_params=params(20),
    )(dense, live, cd, yl, yr, p_swap, s_swap)
    v_onward, v, _ = lax.optimization_barrier((first, first, od))
    v_far = lax.ppermute(v_onward, RING, onward)
    gram = pl.pallas_call(
        link_kernel,
        out_shape=full,
        in_specs=[VM] * 2,
        out_specs=VM,
        scratch_shapes=[own16],
        input_output_aliases={0: 0},
        cost_estimate=cost(1),
        compiler_params=params(20),
    )(gram, v)
    part, g, gram, far_live, _ = pl.pallas_call(
        cross_kernel,
        out_shape=(
            shape((ROWS, BS, PANEL), BF16),
            shape((OWN, GW), F32),
            full,
            shape((16, OWN), F32),
            shape((OWN, WIDE), BF16),
        ),
        in_specs=[VM] * 9,
        out_specs=(HBM, VM, VM, VM, VM),
        scratch_shapes=[own16] * 3
        + [
            pltpu.VMEM((ROWS, BS, PANEL), BF16),
            DMA((ROWS,)),
        ],
        input_output_aliases={6: 2, 7: 4},
        cost_estimate=cost(300),
        compiler_params=params(20),
    )(dense, sd, live, cd, yl, yr, gram, od, p_cross)
    return pl.pallas_call(
        last_kernel,
        out_shape=shape((ROWS, BS, PANEL), BF16),
        in_specs=[VM] * 6 + [HBM],
        out_specs=HBM,
        input_output_aliases={6: 0},
        scratch_shapes=[
            own16,
            own16,
            pltpu.VMEM((OWN, GW), BF16),
            pltpu.VMEM((ROWS, BS, PANEL), BF16),
            DMA((ROWS,)),
        ],
        cost_estimate=cost(1),
        compiler_params=params(20),
    )(dense, live, g, gram, far_live, v_far, part)


def solution(mesh):
    in_specs = (
        P(("groups", "rows", "cols"), None, None),
        P(("groups", "rows", "cols"), None),
        P(("groups", "rows", "cols")),
    )
    out_specs = P(("groups", "rows", "cols"), None, None)
    return jax.shard_map(body, mesh=mesh, in_specs=in_specs, out_specs=out_specs, check_vma=False)
```
